512 devices in a mesh: snap: 64 (over z, y_lo, core), feat: 8 (over y_hi, x).
Axes of the slice: x: 4, y: 4 (y_hi: 2, y_lo: 2; y = y_hi * 2 + y_lo), z: 16, core: 2. Of those that a mesh axis runs over, the one named last changes fastest.
Arguments:
- snapshots: bfloat16 [9728, 8192], P('snap', 'feat'), may hold values from -4.4 to 4.4
- spread: bfloat16 [9728], P('snap'), may hold values from 0.14941406 to 0.5
- start_vectors: float32 [9728, 64], P('snap'), may hold values from -40 to 40
Outputs:
- basis: float32 [9728, 64], P('snap')
The draws below stay inside these ranges and needn't reach their ends.
All inputs are finite; a program needn't handle non-finite values.
Results may differ from the reference program's by a relative error of at most 0.0013.
Values may be sent and summed in bfloat16 or wider, within the bound.
A program may use at most 64 MiB of HBM per device.

```python
import math
import jax
import jax.numpy as jnp
from jax import lax

S_DEV = 152
F = 8192
NV = 64
ITERS = 2
M = 9728
N_SNAP = 64


def draw_times(key):
    return jax.random.uniform(jax.random.fold_in(key, 5), (M,), jnp.float32)


def draw_snapshots(key, part):
    sample_times = draw_times(key)
    key = jax.random.fold_in(key, 11)
    rate_key, phase_key, noise_key = jax.random.split(key, 3)
    frequencies = 2.0 * math.pi * jnp.exp(jax.random.uniform(rate_key, (F,), jnp.float32, 0.0, math.log(100.0)))
    phases = jax.random.uniform(phase_key, (F,), jnp.float32, -math.pi, math.pi)
    noise_draw = jnp.clip(jax.random.normal(noise_key, (M, F), jnp.float32), -4.0, 4.0)
    position = jnp.arange(F, dtype=jnp.float32) / F - 0.5
    amplitudes = jnp.exp(math.log(3.0) * position)
    noise_level = 0.15
    signal = jnp.cos(sample_times[:, None] * frequencies[None, :] + phases[None, :])
    return (amplitudes[None, :] * (signal + noise_level * noise_draw)).astype(jnp.bfloat16)


def draw_start_vectors(key, part):
    sample_times = draw_times(key)
    key = jax.random.fold_in(key, 23)
    noise_key, row_key, column_key = jax.random.split(key, 3)
    orders = jnp.arange(NV, dtype=jnp.float32)
    smooth = jnp.cos(math.pi * sample_times[:, None] * orders[None, :])
    column_scale = jnp.exp(jax.random.uniform(column_key, (NV,), jnp.float32, 0.0, math.log(2.0)))
    noise = 0.1 * jnp.clip(jax.random.normal(noise_key, (M, NV), jnp.float32), -3.0, 3.0)
    row_scale = jnp.exp(jax.random.uniform(row_key, (M,), jnp.float32, 0.0, math.log(10.0)))
    return (smooth + noise) * row_scale[:, None] * column_scale[None, :]


def levels(stream_key, extent, shards, low, top_value):
    level = 1.0
    for dim, parts in shards:
        steps = jax.random.uniform(jax.random.fold_in(jax.random.fold_in(stream_key, 6), dim), (parts,), jnp.float32, low / len(shards), top_value / len(shards))
        level = level * jnp.repeat(jnp.exp(steps), extent[dim] // parts).reshape((-1,) + (1,) * (len(extent) - 1 - dim))
    return level


def setup_inputs(seed: int = 0) -> dict:
    streams_of = jax.random.split(jax.random.key(seed), 4)
    snapshots = draw_snapshots(jax.random.fold_in(streams_of[3], 71), 0)
    spread = jnp.clip(jnp.exp(math.log(0.5) - 1.2078867 * jax.random.uniform(streams_of[1], (M,), jnp.float32) ** levels(streams_of[1], (M,), ((0, 64),), -0.2, 0.2)), 0.14941406, 0.5).astype(jnp.bfloat16)
    start_vectors = draw_start_vectors(jax.random.fold_in(streams_of[3], 71), 0)
    return {"snapshots": snapshots, "spread": spread, "start_vectors": start_vectors}


def reference(snapshots, spread, start_vectors):
    values = snapshots.astype(jnp.float32)
    square_norms = lax.optimization_barrier(jnp.sum(values * values, axis=1))
    widths = spread.astype(jnp.float32)
    row_values = values.reshape(N_SNAP, S_DEV, F)
    row_norms = square_norms.reshape(N_SNAP, S_DEV)
    row_widths = widths.reshape(N_SNAP, S_DEV)

    def kernel_rows(pieces):
        block_values, block_norms, block_widths = pieces
        inner = jnp.dot(block_values, values.T, precision=lax.Precision.HIGHEST)
        distances = block_norms[:, None] + square_norms[None, :] - 2.0 * inner
        exponent = -(distances / (block_widths[:, None] * widths[None, :])) / F
        kernel_block = jnp.exp(exponent).astype(jnp.bfloat16)
        return (kernel_block, lax.optimization_barrier(jnp.sum(kernel_block.astype(jnp.float32), axis=1)))
    kernel, degree = lax.map(kernel_rows, (row_values, row_norms, row_widths))
    kernel = kernel.reshape(M, M)
    degree = degree.reshape(M)
    scale = 1.0 / jnp.sqrt(degree)
    vectors = start_vectors
    for iteration in range(ITERS):
        weighted = (scale[:, None] * vectors).astype(jnp.bfloat16)
        image = jnp.dot(kernel.astype(jnp.float32), weighted.astype(jnp.float32), preferred_element_type=jnp.float32)
        mixed = 0.5 * (vectors + scale[:, None] * image)
        gram_matrix = jnp.dot(mixed.T, mixed, precision=lax.Precision.HIGHEST) / M
        lower_factor = jnp.linalg.cholesky(gram_matrix)
        vectors = jax.scipy.linalg.solve_triangular(lower_factor, mixed.T, lower=True).T
    return vectors
```

```python
import functools

import jax
import jax.numpy as jnp
from jax import lax
from jax.experimental import pallas as pl
from jax.experimental.pallas import tpu as pltpu
from jax.sharding import PartitionSpec as P

ITERS = 2
Z = 16
Q = 4
NF = 8
NX = 4
HOPS = 4
ROWS = 152
PAD = 160
WIDE = Q * PAD
NV = 64
FEATURES = 8192
TOTAL = Z * Q * ROWS
F32 = jnp.float32
BF16 = jnp.bfloat16
HIGHEST = lax.Precision.HIGHEST


class Ids:
    def __init__(self):
        self.count = 0

    def take(self, number=1):
        first = self.count
        self.count += number
        return first


def dot_nt(a, b, precision=None):
    return lax.dot_general(
        a, b, (((1,), (1,)), ((), ())), precision=precision, preferred_element_type=F32
    )


def dot_nn(a, b, precision=None):
    return lax.dot_general(
        a, b, (((1,), (0,)), ((), ())), precision=precision, preferred_element_type=F32
    )


def eye(rows, columns):
    row = lax.broadcasted_iota(jnp.int32, (rows, columns), 0)
    column = lax.broadcasted_iota(jnp.int32, (rows, columns), 1)
    return row == column


def column_of(row):
    n = row.shape[1]
    return jnp.sum(jnp.where(eye(n, n), row, 0.0), axis=1, keepdims=True)


def row_norms(block):
    wide = block.astype(F32)
    return jnp.sum(wide * wide, axis=1, keepdims=True)


def inverse_factor(gram):
    n = gram.shape[0]
    both = jnp.concatenate([gram, eye(n, n).astype(F32)], axis=1)
    rows = lax.broadcasted_iota(jnp.int32, (n, 1), 0)
    for j in range(n - 1):
        pivot_row = both[j : j + 1, :]
        factor = both[:, j : j + 1] * (1.0 / pivot_row[:, j : j + 1])
        both = both - jnp.where(rows > j, factor, 0.0) * pivot_row
    diagonal = jnp.sum(jnp.where(eye(n, n), both[:, :n], 0.0), axis=1, keepdims=True)
    return both[:, n:] * lax.rsqrt(diagonal)


def count_ids():
    ids = Ids()
    names = {}
    names["up"] = ids.take(HOPS + 1)
    names["down"] = ids.take(HOPS + 1)
    names["across"] = ids.take(HOPS + 1)
    names["mate"] = ids.take(HOPS + 1)
    names["mate2"] = ids.take(HOPS + 1)
    names["x_send"] = ids.take(9)
    names["x_recv"] = ids.take(9)
    names["y"] = ids.take(2)
    names["gather"] = ids.take((ITERS + 1) * 8)
    names["parts"] = ids.take((ITERS + 1) * 5)
    names["feat"] = ids.take((ITERS + 1) * 8)
    names["gram_q"] = ids.take(ITERS * 4)
    names["gram_z"] = ids.take(ITERS * 2)
    names["gram_f"] = ids.take(ITERS * 8)
    return names, ids.count


NAMES, N_IDS = count_ids()


def kernel(
    x_ref,
    spread_ref,
    start_ref,
    out_ref,
    cbuf,
    rbuf,
    pbuf,
    xbuf,
    ysend,
    yrecv,
    keep,
    kq,
    k0,
    width_src,
    width_c,
    width_r,
    width_0,
    w_src,
    w_c,
    w_r,
    w_0,
    d_src,
    dc_src,
    d_r,
    d_c,
    d_f,
    i_src,
    ic_src,
    i_r,
    i_c,
    i_f,
    g_q,
    g_zsrc,
    g_z,
    g_f,
    send_sem,
    recv_sem,
):
    snap = lax.axis_index("snap")
    f = lax.axis_index("feat")
    z = snap // Q
    q = snap % Q
    x = f % NX
    yh = f // NX
    k = f + 1
    r_off = (k + 1) // 2
    c_off = k // 2
    q_across = (q + 2) % Q
    q_mate = q + 1 - 2 * (q % 2)
    q_both = (q_mate + 2) % Q

    def at(zz, qq, ff):
        return {"snap": ((zz + Z) % Z) * Q + qq, "feat": ff}

    pending = []

    def copy(src, dst, name, send, recv, device, when=None):
        made = pltpu.make_async_remote_copy(
            src_ref=src,
            dst_ref=dst,
            send_sem=send_sem.at[NAMES[name] + send],
            recv_sem=recv_sem.at[NAMES[name if name != "x_send" else "x_recv"] + recv],
            device_id=device,
            device_id_type=pl.DeviceIdType.MESH,
        )
        if when is None:
            made.start()
        else:
            pl.when(when)(made.start)
        pending.append((made, when))

    def arrived(dst, name, recv):
        pltpu.make_async_remote_copy(
            src_ref=dst,
            dst_ref=dst,
            send_sem=send_sem.at[NAMES[name]],
            recv_sem=recv_sem.at[NAMES[name] + recv],
            device_id=at(z, q_mate, f),
            device_id_type=pl.DeviceIdType.MESH,
        ).wait_recv()

    barrier = pltpu.get_barrier_semaphore()
    first = f == 0
    not_first = f != 0

    def greet(device):
        pl.semaphore_signal(
            barrier, inc=1, device_id=device, device_id_type=pl.DeviceIdType.MESH
        )

    greet(at(z + 1, q, f))
    greet(at(z - 1, q, f))
    for i in range(1, Q):
        greet(at(z, (q + i) % Q, f))
    for i in range(1, NF):
        greet(at(z, q, (f + i) % NF))
    for i in range(Q):
        greet(at(z + r_off, i, f))
        greet(at(z - r_off, i, f))
    greet(at(z + 8 + f, q, f))

    @pl.when(not_first)
    def _():
        greet(at(z + c_off, q, f))
        greet(at(z - c_off, q, f))
        greet(at(z + f, q, f))

    cbuf[0, :ROWS, :] = x_ref[...]
    cbuf[0, ROWS:, :] = jnp.zeros((PAD - ROWS, cbuf.shape[2]), BF16)
    lane = lax.broadcasted_iota(jnp.int32, (1, PAD), 1)
    width_src[...] = jnp.broadcast_to(
        jnp.concatenate(
            [spread_ref[...].astype(F32), jnp.ones((1, PAD - ROWS), F32)], axis=1
        ),
        (8, PAD),
    )
    pl.semaphore_wait(barrier, 2 + 3 + 7 + 8 + 1 + 3 * not_first.astype(jnp.int32))

    def spread_out(src, c_dst, r_dst, z_dst, base):
        for i in range(Q):
            copy(src, r_dst.at[q], "gather", base + i, base + q, at(z - r_off, i, f))
        copy(src, c_dst, "gather", base + 4, base + 4, at(z + c_off, q, f), not_first)

        @pl.when(first)
        def _():
            c_dst[...] = src[...]
            z_dst[q] = src[...]

        for i in range(1, Q):
            copy(src, z_dst.at[q], "gather", base + 4 + i, base + 4 + i, at(z, (q + i) % Q, f), first)

    def spread_in(c_dst, r_dst, z_dst, base):
        for i in range(Q):
            arrived(r_dst.at[i], "gather", base + i)
        pl.when(not_first)(lambda: arrived(c_dst, "gather", base + 4))

        @pl.when(first)
        def _():
            for i in range(1, Q):
                arrived(z_dst.at[(q + Q - i) % Q], "gather", base + 4 + i)

    copy(cbuf.at[0], cbuf.at[1], "up", 1, 1, at(z + 1, q, f))
    copy(cbuf.at[0], rbuf.at[1, q], "down", 1, 1, at(z - 1, q, f))
    copy(cbuf.at[0], rbuf.at[0, q], "across", 0, 0, at(z, q_across, f))
    copy(cbuf.at[0], rbuf.at[0, q], "mate", 0, 0, at(z, q_mate, f))
    rbuf[0, q] = cbuf[0]
    spread_out(width_src, width_c, width_r, width_0, 0)

    def rows_arrive(h):
        arrived(rbuf.at[h, q_across], "across", h)
        copy(rbuf.at[h, q_across], rbuf.at[h, q_across], "mate2", h, h, at(z, q_mate, f))

    def tile_parts(h):
        arrived(rbuf.at[h, q_mate], "mate", h)
        arrived(rbuf.at[h, q_both], "mate2", h)
        wide_row = lax.broadcasted_iota(jnp.int32, (PAD, WIDE), 0)
        wide_lane = lax.broadcasted_iota(jnp.int32, (PAD, WIDE), 1)
        picked = jnp.zeros((PAD, WIDE), F32)
        for i in range(Q):
            picked = jnp.where(wide_lane == wide_row + i * PAD, row_norms(rbuf[h, i]), picked)
        r_norms = jnp.sum(picked, axis=0, keepdims=True)
        r_block = rbuf[h].reshape(WIDE, rbuf.shape[3])
        for kk, c in [(0, 0)] if h == 0 else [(2 * h - 1, h - 1), (2 * h, h)]:
            inner = dot_nt(cbuf[c], r_block)
            pbuf[kk] = (row_norms(cbuf[c]) + r_norms - 2.0 * inner).astype(BF16)
            owner, slot = (0, 2) if kk == 0 else ((kk - 1) % NX, (kk - 1) // NX)
            source = (x - owner + NX - 1) % NX
            copy(
                pbuf.at[kk],
                xbuf.at[slot, source % 3],
                "x_send",
                kk,
                slot * 3 + source % 3,
                at(z, q, yh * NX + owner),
                x != owner,
            )

    def sum_x(kk):
        owner, slot = (0, 2) if kk == 0 else ((kk - 1) % NX, (kk - 1) // NX)
        last = 0 if kk == 0 else slot
        kind = 1 if kk == 0 else 0

        @pl.when(x == owner)
        def _():
            for i in range(3):
                arrived(xbuf.at[slot, i], "x_recv", slot * 3 + i)
            total = pbuf[kk].astype(F32)
            for i in range(3):
                total = total + xbuf[slot, i].astype(F32)

            @pl.when(yh == last)
            def _():
                keep[kind] = total

            @pl.when(yh != last)
            def _():
                ysend[kind] = total.astype(BF16)

        copy(
            ysend.at[kind],
            yrecv.at[kind],
            "y",
            kind,
            kind,
            at(z, q, (f + NX) % NF),
            (x == owner) & (yh != last),
        )

    for step in range(HOPS + 3):
        if 1 <= step <= HOPS:
            h = step
            arrived(rbuf.at[h, q], "down", h)
            if h < HOPS:
                copy(rbuf.at[h, q], rbuf.at[h + 1, q], "down", h + 1, h + 1, at(z - 1, q, f))
            copy(rbuf.at[h, q], rbuf.at[h, q], "across", h, h, at(z, q_across, f))
            copy(rbuf.at[h, q], rbuf.at[h, q], "mate", h, h, at(z, q_mate, f))
            arrived(cbuf.at[h], "up", h)
            if h < HOPS:
                copy(cbuf.at[h], cbuf.at[h + 1], "up", h + 1, h + 1, at(z + 1, q, f))
        if 1 <= step <= HOPS + 1:
            rows_arrive(step - 1)
            tile_parts(step - 1)
        if step >= 2:
            h = step - 2
            for kk in [0] if h == 0 else [2 * h - 1, 2 * h]:
                sum_x(kk)

    spread_in(width_c, width_r, width_0, 0)

    def kernel_blocks(total, c_width, r_width, dst):
        c_column = column_of(c_width)
        row = lax.broadcasted_iota(jnp.int32, (PAD, PAD), 0)
        column = lax.broadcasted_iota(jnp.int32, (PAD, PAD), 1)
        inside = (row < ROWS) & (column < ROWS)
        for i in range(Q):
            distance = total[:, i * PAD : (i + 1) * PAD]
            exponent = -(distance / (c_column * r_width[i, :1, :])) / FEATURES
            dst[i] = jnp.where(inside, jnp.exp(exponent), 0.0).astype(BF16)

    arrived(yrecv.at[0], "y", 0)
    kernel_blocks(keep[0] + yrecv[0].astype(F32), width_c[:1, :], width_r, kq)

    @pl.when(first)
    def _():
        arrived(yrecv.at[1], "y", 1)
        kernel_blocks(keep[1] + yrecv[1].astype(F32), width_src[:1, :], width_0, k0)

    def product(index, height, c_rows, r_rows, z_rows, src, c_src, got_r, got_c, got_f):
        for i in range(Q):
            src[i] = dot_nn(c_rows, kq[i])[:height]
        part = dot_nt(r_rows(0), kq[0])
        for i in range(1, Q):
            part = part + dot_nt(r_rows(i), kq[i])
        part = part[:height]

        @pl.when(not_first)
        def _():
            c_src[...] = part

        @pl.when(first)
        def _():
            own = part
            for i in range(Q):
                own = own + dot_nt(z_rows(i), k0[i])[:height]
            got_c[...] = own

        @pl.when(f == NF - 1)
        def _():
            got_c[...] = jnp.zeros_like(got_c)

        base = index * 5
        middle = not_first & (f != NF - 1)
        for i in range(Q):
            copy(src.at[i], got_r.at[q], "parts", base + i, base + q, at(z + r_off, i, f))
        copy(c_src, got_c, "parts", base + 4, base + 4, at(z - c_off, q, f), middle)
        for i in range(Q):
            arrived(got_r.at[i], "parts", base + i)
        pl.when(middle)(lambda: arrived(got_c, "parts", base + 4))
        total = got_c[...]
        for i in range(Q):
            total = total + got_r[i]
        return sum_feat(total, got_f, "feat", index * 8)

    def sum_feat(total, got_f, name, base):
        got_f[f] = total
        for i in range(1, NF):
            copy(got_f.at[f], got_f.at[f], name, base + i, base + i, at(z, q, (f + i) % NF))
        for i in range(1, NF):
            arrived(got_f.at[(f + NF - i) % NF], name, base + i)
        total = got_f[0]
        for i in range(1, NF):
            total = total + got_f[i]
        return total

    ones = jnp.ones((16, PAD), BF16)
    degree = product(
        0, 8, ones, lambda i: ones, lambda i: ones, d_src, dc_src, d_r, d_c, d_f
    )[:1]
    scale = jnp.where(lane < ROWS, 1.0 / jnp.sqrt(jnp.where(lane < ROWS, degree, 1.0)), 0.0)

    start = jnp.concatenate(
        [start_ref[...], jnp.zeros((PAD - ROWS, NV), F32)], axis=0
    )
    vectors = dot_nt(eye(NV, NV).astype(F32), start, HIGHEST)
    for it in range(ITERS):
        w_src[it] = (scale * vectors).astype(BF16)
        spread_out(w_src.at[it], w_c.at[it], w_r.at[it], w_0.at[it], 8 * (it + 1))
        spread_in(w_c.at[it], w_r.at[it], w_0.at[it], 8 * (it + 1))
        image = product(
            it + 1,
            NV,
            w_c[it],
            lambda i, it=it: w_r[it, i],
            lambda i, it=it: w_0[it, i],
            i_src.at[it],
            ic_src.at[it],
            i_r.at[it],
            i_c.at[it],
            i_f.at[it],
        )
        mixed = 0.5 * (vectors + scale * image)
        g_q[it, q] = dot_nt(mixed, mixed, HIGHEST)
        for i in range(1, Q):
            copy(g_q.at[it, q], g_q.at[it, q], "gram_q", 4 * it + i, 4 * it + i, at(z, (q + i) % Q, f))
        for i in range(1, Q):
            arrived(g_q.at[it, (q + Q - i) % Q], "gram_q", 4 * it + i)
        here = g_q[it, 0]
        for i in range(1, Q):
            here = here + g_q[it, i]
        g_zsrc[it] = here

        @pl.when(first)
        def _():
            g_z[it, 0] = here

        copy(g_zsrc.at[it], g_z.at[it, 0], "gram_z", 2 * it, 2 * it, at(z - f, q, f), not_first)
        copy(g_zsrc.at[it], g_z.at[it, 1], "gram_z", 2 * it + 1, 2 * it + 1, at(z + 8 - f, q, f))
        pl.when(not_first)(lambda it=it: arrived(g_z.at[it, 0], "gram_z", 2 * it))
        arrived(g_z.at[it, 1], "gram_z", 2 * it + 1)
        gram = sum_feat(g_z[it, 0] + g_z[it, 1], g_f.at[it], "gram_f", 8 * it)
        inverse = inverse_factor(gram / TOTAL)
        vectors = dot_nn(inverse, mixed, HIGHEST)

    out_ref[...] = dot_nt(eye(PAD, PAD).astype(F32), vectors, HIGHEST)[:ROWS]
    for made, when in pending:
        if when is None:
            made.wait_send()
        else:
            pl.when(when)(made.wait_send)


def per_device(snapshots, spread, start_vectors):
    depth = snapshots.shape[1]
    vmem = pltpu.VMEM
    shapes = [
        vmem((HOPS + 1, PAD, depth), BF16),
        vmem((HOPS + 1, Q, PAD, depth), BF16),
        vmem((9, PAD, WIDE), BF16),
        vmem((3, 3, PAD, WIDE), BF16),
        vmem((2, PAD, WIDE), BF16),
        vmem((2, PAD, WIDE), BF16),
        vmem((2, PAD, WIDE), F32),
        vmem((Q, PAD, PAD), BF16),
        vmem((Q, PAD, PAD), BF16),
        vmem((8, PAD), F32),
        vmem((8, PAD), F32),
        vmem((Q, 8, PAD), F32),
        vmem((Q, 8, PAD), F32),
        vmem((ITERS, NV, PAD), BF16),
        vmem((ITERS, NV, PAD), BF16),
        vmem((ITERS, Q, NV, PAD), BF16),
        vmem((ITERS, Q, NV, PAD), BF16),
        vmem((Q, 8, PAD), F32),
        vmem((8, PAD), F32),
        vmem((Q, 8, PAD), F32),
        vmem((8, PAD), F32),
        vmem((NF, 8, PAD), F32),
        vmem((ITERS, Q, NV, PAD), F32),
        vmem((ITERS, NV, PAD), F32),
        vmem((ITERS, Q, NV, PAD), F32),
        vmem((ITERS, NV, PAD), F32),
        vmem((ITERS, NF, NV, PAD), F32),
        vmem((ITERS, Q, NV, NV), F32),
        vmem((ITERS, NV, NV), F32),
        vmem((ITERS, 2, NV, NV), F32),
        vmem((ITERS, NF, NV, NV), F32),
        pltpu.SemaphoreType.DMA((N_IDS,)),
        pltpu.SemaphoreType.DMA((N_IDS,)),
    ]
    return pl.pallas_call(
        kernel,
        out_shape=jax.ShapeDtypeStruct(start_vectors.shape, F32),
        in_specs=[pl.BlockSpec(memory_space=pltpu.VMEM)] * 3,
        out_specs=pl.BlockSpec(memory_space=pltpu.VMEM),
        scratch_shapes=shapes,
        compiler_params=pltpu.CompilerParams(
            collective_id=0, has_side_effects=True, vmem_limit_bytes=40 * 1024 * 1024
        ),
        cost_estimate=pl.CostEstimate(
            flops=4_000_000_000, bytes_accessed=400_000, transcendentals=200_000
        ),
        name="subspace",
    )(snapshots, spread.reshape(1, -1), start_vectors)


def solution(mesh):
    return jax.shard_map(
        per_device,
        mesh=mesh,
        in_specs=(P("snap", "feat"), P("snap"), P("snap", None)),
        out_specs=P("snap", None),
        check_vma=False,
    )
```

```python
import jax
import jax.numpy as jnp
from jax import lax
from jax.experimental import pallas as pl
from jax.experimental.pallas import tpu as pltpu
from jax.sharding import PartitionSpec as P

Z = 16
Q = 4
NF = 8
NX = 4
HOPS = 4
HALVES = 2
ROWS = 152
PAD = 160
WIDE = 4 * PAD
NV = 64
FEATURES = 8192
TOTAL = Z * Q * ROWS
F32 = jnp.float32
BF16 = jnp.bfloat16
HIGHEST = lax.Precision.HIGHEST
R_OFF = (0, 1, 1, 2, 2, 3, 3, 3, 4)
C_OFF = (0, 0, 1, 1, 2, 2, 3, 4, 4)


def dot_nt(a, b, precision=None):
    return lax.dot_general(
        a, b, (((1,), (1,)), ((), ())), precision=precision, preferred_element_type=F32
    )


def dot_nn(a, b, precision=None):
    return lax.dot_general(
        a, b, (((1,), (0,)), ((), ())), precision=precision, preferred_element_type=F32
    )


def eye(n):
    row = lax.broadcasted_iota(jnp.int32, (n, n), 0)
    column = lax.broadcasted_iota(jnp.int32, (n, n), 1)
    return row == column


def column_of(row):
    return jnp.sum(jnp.where(eye(row.shape[1]), row, 0.0), axis=1, keepdims=True)


def row_of(column):
    return jnp.sum(jnp.where(eye(column.shape[0]), column, 0.0), axis=0, keepdims=True)


def inverse_factor(gram):
    n = gram.shape[0]
    both = jnp.concatenate([gram, eye(n).astype(F32)], axis=1)
    rows = lax.broadcasted_iota(jnp.int32, (n, 1), 0)
    for j in range(n - 1):
        pivot_row = both[j : j + 1, :]
        factor = both[:, j : j + 1] * (1.0 / pivot_row[:, j : j + 1])
        both = both - jnp.where(rows > j, factor, 0.0) * pivot_row
    diagonal = jnp.sum(jnp.where(eye(n), both[:, :n], 0.0), axis=1, keepdims=True)
    return both[:, n:] * lax.rsqrt(diagonal)


def count_ids():
    sizes = {
        "up": (HOPS + 1) * HALVES,
        "down": (HOPS + 1) * HALVES,
        "across": (HOPS + 1) * HALVES,
        "mate": (HOPS + 1) * HALVES,
        "x": 9,
        "y": 2,
        "gather": 3 * 5,
        "parts": 3 * 4,
        "feat": 3 * 8,
        "gram_q": 2 * 4,
        "gram_z": 2 * 2,
        "gram_f": 2 * 8,
    }
    names, count = {}, 0
    for name, size in sizes.items():
        names[name] = count
        count += size
    return names, count


NAMES, N_IDS = count_ids()


def kernel(
    x_ref,
    spread_ref,
    start_ref,
    out_ref,
    cbuf,
    rbuf,
    pbuf,
    xbuf,
    ysend,
    yrecv,
    keep,
    kq,
    k0,
    width_src,
    width_c,
    width_r,
    width_0,
    w_src,
    w_c,
    w_r,
    w_0,
    d_rsrc,
    d_csrc,
    d_r,
    d_c,
    d_f,
    i_rsrc,
    i_csrc,
    i_r,
    i_c,
    i_f,
    g_q,
    g_zsrc,
    g_z,
    g_f,
    send_sem,
    recv_sem,
):
    snap = lax.axis_index("snap")
    f = lax.axis_index("feat")
    z = snap // Q
    q = snap % Q
    y = q // 2
    c = q % 2
    x = f % NX
    yh = f // NX
    k = f + 1
    is_7 = (k == 7).astype(jnp.int32)
    r_off = (k + 1) // 2 - is_7
    c_off = k // 2 + is_7
    first = f == 0
    not_first = f != 0
    has_c = not_first & (f != NF - 1)
    half_depth = cbuf.shape[4]

    def at(zz, yy, cc, ff):
        return {"snap": ((zz + Z) % Z) * Q + yy * 2 + cc, "feat": ff}

    across = at(z, 1 - y, c, f)
    mate = at(z, y, 1 - c, f)
    pending = []

    def copy(src, dst, name, send, recv, device, when=None):
        made = pltpu.make_async_remote_copy(
            src_ref=src,
            dst_ref=dst,
            send_sem=send_sem.at[NAMES[name] + send],
            recv_sem=recv_sem.at[NAMES[name] + recv],
            device_id=device,
            device_id_type=pl.DeviceIdType.MESH,
        )
        if when is None:
            made.start()
        else:
            pl.when(when)(made.start)
        pending.append((made, when))

    def arrived(dst, name, recv):
        pltpu.make_async_remote_copy(
            src_ref=dst,
            dst_ref=dst,
            send_sem=send_sem.at[NAMES[name]],
            recv_sem=recv_sem.at[NAMES[name] + recv],
            device_id=mate,
            device_id_type=pl.DeviceIdType.MESH,
        ).wait_recv()

    barrier = pltpu.get_barrier_semaphore()
    near = [at(z + 1, y, c, f), at(z - 1, y, c, f), across, mate]
    near += [at(z, y, c, yh * NX + (x + i) % NX) for i in range(1, NX)]
    near += [at(z, y, c, (f + NX) % NF)]
    for device in near:
        pl.semaphore_signal(
            barrier, inc=1, device_id=device, device_id_type=pl.DeviceIdType.MESH
        )
    for half in range(HALVES):
        part = x_ref[:, half * half_depth : (half + 1) * half_depth]
        rest = jnp.zeros((PAD - ROWS, half_depth), BF16)
        cbuf[0, c, half, :ROWS, :] = part
        cbuf[0, c, half, ROWS:, :] = rest
        rbuf[0, y, half, :ROWS, :] = part
        rbuf[0, y, half, ROWS:, :] = rest
    lane = lax.broadcasted_iota(jnp.int32, (1, PAD), 1)
    width_src[...] = jnp.broadcast_to(
        jnp.concatenate(
            [spread_ref[...].astype(F32), jnp.ones((1, PAD - ROWS), F32)], axis=1
        ),
        (8, PAD),
    )
    pl.semaphore_wait(barrier, len(near))

    def send_down(h, half):
        src = rbuf.at[h, y, half]
        if h < HOPS:
            number = (h + 1) * HALVES + half
            copy(src, rbuf.at[h + 1, y, half], "down", number, number, at(z - 1, y, c, f))
        number = h * HALVES + half
        copy(src, rbuf.at[h, y, half], "across", number, number, across)

    def send_up(h, half):
        src = cbuf.at[h, c, half]
        if h < HOPS:
            number = (h + 1) * HALVES + half
            copy(src, cbuf.at[h + 1, c, half], "up", number, number, at(z + 1, y, c, f))
        number = h * HALVES + half
        copy(src, cbuf.at[h, c, half], "mate", number, number, mate)

    def travel(h, halves=range(HALVES)):
        for half in halves:
            number = h * HALVES + half
            if h > 0:
                arrived(rbuf.at[h, y, half], "down", number)
            send_down(h, half)
            if h > 0:
                arrived(cbuf.at[h, c, half], "up", number)
            send_up(h, half)

    def norms(ref, h, i):
        total = jnp.zeros((PAD, 1), F32)
        for half in range(HALVES):
            wide = ref[h, i, half].astype(F32)
            total = total + jnp.sum(wide * wide, axis=1, keepdims=True)
        return total

    def owner_of(kk):
        return (0, 0, 2) if kk == 0 else ((kk - 1) % NX, (kk - 1) // NX, (kk - 1) // NX)

    def make_tile(kk):
        r, h = R_OFF[kk], C_OFF[kk]
        c_norms = [norms(cbuf, h, j) for j in range(2)]
        r_norms = [row_of(norms(rbuf, r, i)) for i in range(2)]
        blocks = []
        for j in range(2):
            for i in range(2):
                inner = dot_nt(cbuf[h, j, 0], rbuf[r, i, 0])
                for half in range(1, HALVES):
                    inner = inner + dot_nt(cbuf[h, j, half], rbuf[r, i, half])
                blocks.append(c_norms[j] + r_norms[i] - 2.0 * inner)
        pbuf[kk] = jnp.concatenate(blocks, axis=1).astype(BF16)
        owner, _, slot = owner_of(kk)
        source = (x - owner + NX - 1) % NX % 3
        copy(
            pbuf.at[kk],
            xbuf.at[slot, source],
            "x",
            kk,
            slot * 3 + source,
            at(z, y, c, yh * NX + owner),
            x != owner,
        )

    def sum_x(kk):
        owner, last, slot = owner_of(kk)
        kind = 1 if kk == 0 else 0

        @pl.when(x == owner)
        def _():
            for i in range(3):
                arrived(xbuf.at[slot, i], "x", slot * 3 + i)
            total = pbuf[kk].astype(F32)
            for i in range(3):
                total = total + xbuf[slot, i].astype(F32)

            @pl.when(yh == last)
            def _():
                keep[kind] = total

            @pl.when(yh != last)
            def _():
                ysend[kind] = total.astype(BF16)

        copy(
            ysend.at[kind],
            yrecv.at[kind],
            "y",
            kind,
            kind,
            at(z, y, c, (f + NX) % NF),
            (x == owner) & (yh != last),
        )

    def rows_in(h):
        for half in range(HALVES):
            arrived(rbuf.at[h, 1 - y, half], "across", h * HALVES + half)

    def columns_in(h):
        for half in range(HALVES):
            arrived(cbuf.at[h, 1 - c, half], "mate", h * HALVES + half)

    def spread_out(src, c_dst, r_dst, z_dst, base):
        for i in range(2):
            copy(src, r_dst.at[y], "gather", base + i, base + y, at(z - r_off, i, c, f))
        for i in range(2):
            number = base + 2 + i
            copy(src, c_dst.at[c], "gather", number, base + 2 + c, at(z + c_off, y, i, f), not_first)

        copy(src, c_dst.at[c], "gather", base + 2, base + 2 + c, mate, first)
        copy(src, z_dst.at[y], "gather", base + 4, base + 4, across, first)

        @pl.when(first)
        def _():
            c_dst[c] = src[...]
            z_dst[y] = src[...]

    def spread_in(c_dst, r_dst, z_dst, base):
        for i in range(2):
            arrived(r_dst.at[i], "gather", base + i)

        @pl.when(not_first)
        def _():
            for i in range(2):
                arrived(c_dst.at[i], "gather", base + 2 + i)

        @pl.when(first)
        def _():
            arrived(c_dst.at[1 - c], "gather", base + 2 + 1 - c)
            arrived(z_dst.at[1 - y], "gather", base + 4)

    travel(0)
    travel(1)
    columns_in(0)
    rows_in(0)
    make_tile(0)
    travel(2)
    rows_in(1)
    make_tile(1)
    columns_in(1)
    make_tile(2)
    travel(3)
    sum_x(0)
    rows_in(2)
    make_tile(3)
    columns_in(2)
    make_tile(4)
    travel(4, range(HALVES // 2))
    sum_x(1)
    sum_x(2)
    rows_in(3)
    make_tile(5)
    columns_in(3)
    make_tile(6)
    travel(4, range(HALVES // 2, HALVES))
    sum_x(3)
    sum_x(4)
    columns_in(4)
    make_tile(7)
    rows_in(4)
    make_tile(8)
    spread_out(width_src, width_c, width_r, width_0, 0)
    sum_x(5)
    sum_x(6)
    spread_in(width_c, width_r, width_0, 0)
    sum_x(7)
    sum_x(8)

    def kernel_blocks(kind, c_width, r_width, dst):
        row = lax.broadcasted_iota(jnp.int32, (PAD, PAD), 0)
        column = lax.broadcasted_iota(jnp.int32, (PAD, PAD), 1)
        inside = (row < ROWS) & (column < ROWS)
        total = keep[kind] + yrecv[kind].astype(F32)
        for j in range(2):
            c_column = column_of(c_width[j, :1, :])
            for i in range(2):
                b = j * 2 + i
                distance = total[:, b * PAD : (b + 1) * PAD]
                exponent = -(distance / (c_column * r_width[i, :1, :])) / FEATURES
                dst[b] = jnp.where(inside, jnp.exp(exponent), 0.0).astype(BF16)

    @pl.when(first)
    def _():
        arrived(yrecv.at[1], "y", 1)
        kernel_blocks(1, width_c, width_0, k0)

    arrived(yrecv.at[0], "y", 0)
    kernel_blocks(0, width_c, width_r, kq)

    def parts_out(index, height, w_of, r_src, c_src, got_r, got_c):
        base = index * 4
        kind = got_r.dtype
        for i in range(2):
            part = dot_nn(w_of("c", 0), kq[i]) + dot_nn(w_of("c", 1), kq[2 + i])
            r_src[i] = part[:height].astype(kind)
            copy(r_src.at[i], got_r.at[y], "parts", base + i, base + y, at(z + r_off, i, c, f))
        for j in range(2):
            part = dot_nt(w_of("r", 0), kq[2 * j]) + dot_nt(w_of("r", 1), kq[2 * j + 1])

            @pl.when(not_first)
            def _(part=part, j=j):
                c_src[j] = part[:height].astype(kind)

            @pl.when(first)
            def _(part=part, j=j):
                own = part + dot_nt(w_of("0", 0), k0[2 * j]) + dot_nt(w_of("0", 1), k0[2 * j + 1])
                c_src[j] = own[:height].astype(kind)

            copy(c_src.at[j], got_c.at[c], "parts", base + 2 + j, base + 2 + c, at(z - c_off, y, j, f), has_c)
        copy(c_src.at[1 - c], got_c.at[c], "parts", base + 2, base + 2 + c, mate, first)

        @pl.when(first)
        def _():
            got_c[c] = c_src[c]

        @pl.when(f == NF - 1)
        def _():
            got_c[...] = jnp.zeros_like(got_c)

    def parts_in(index, got_r, got_c):
        base = index * 4
        for i in range(2):
            arrived(got_r.at[i], "parts", base + i)

        @pl.when(has_c)
        def _():
            for i in range(2):
                arrived(got_c.at[i], "parts", base + 2 + i)

        pl.when(first)(lambda: arrived(got_c.at[1 - c], "parts", base + 2 + 1 - c))
        total = got_r[0].astype(F32) + got_r[1].astype(F32)
        return total + got_c[0].astype(F32) + got_c[1].astype(F32)

    def feat_out(total, got_f, name, base):
        got_f[f] = total.astype(got_f.dtype)
        for i in range(1, NF):
            copy(got_f.at[f], got_f.at[f], name, base + i, base + i, at(z, y, c, (f + i) % NF))

    def feat_in(got_f, name, base):
        for i in range(1, NF):
            arrived(got_f.at[(f + NF - i) % NF], name, base + i)
        total = got_f[0].astype(F32)
        for i in range(1, NF):
            total = total + got_f[i].astype(F32)
        return total

    def gram_q_out(it, mixed):
        gram = dot_nt(mixed, mixed, HIGHEST)
        g_q[it, q] = jnp.concatenate([gram[: NV // 2], gram[NV // 2 :]], axis=1)
        for i in range(1, Q):
            there = (q + i) % Q
            copy(g_q.at[it, q], g_q.at[it, q], "gram_q", 4 * it + i, 4 * it + i, at(z, there // 2, there % 2, f))

    def gram_q_in(it):
        for i in range(1, Q):
            arrived(g_q.at[it, (q + Q - i) % Q], "gram_q", 4 * it + i)
        here = g_q[it, 0]
        for i in range(1, Q):
            here = here + g_q[it, i]
        g_zsrc[it] = here

        @pl.when(first)
        def _():
            g_z[it, 0] = here

        base = 2 * it
        copy(g_zsrc.at[it], g_z.at[it, 0], "gram_z", base, base, at(z - f, y, c, f), not_first)
        copy(g_zsrc.at[it], g_z.at[it, 1], "gram_z", base + 1, base + 1, at(z + 8 - f, y, c, f))

    def gram_z_in(it):
        pl.when(not_first)(lambda: arrived(g_z.at[it, 0], "gram_z", 2 * it))
        arrived(g_z.at[it, 1], "gram_z", 2 * it + 1)
        feat_out(g_z[it, 0] + g_z[it, 1], g_f.at[it], "gram_f", 8 * it)

    def gram_f_in(it):
        pair = feat_in(g_f.at[it], "gram_f", 8 * it) / TOTAL
        return jnp.concatenate([pair[:, :NV], pair[:, NV:]], axis=0)

    ones = jnp.ones((16, PAD), BF16)
    parts_out(0, 8, lambda kind, i: ones, d_rsrc, d_csrc, d_r, d_c)
    feat_out(parts_in(0, d_r, d_c), d_f, "feat", 0)
    degree = feat_in(d_f, "feat", 0)[:1]
    scale = jnp.where(lane < ROWS, 1.0 / jnp.sqrt(jnp.where(lane < ROWS, degree, 1.0)), 0.0)

    def rows_out(it, vectors):
        w_src[it] = (scale * vectors).astype(BF16)
        spread_out(w_src.at[it], w_c.at[it], w_r.at[it], w_0.at[it], 5 * (it + 1))

    def rows_back(it):
        spread_in(w_c.at[it], w_r.at[it], w_0.at[it], 5 * (it + 1))

        def w_of(kind, i):
            return {"c": w_c, "r": w_r, "0": w_0}[kind][it, i]

        parts_out(it + 1, NV, w_of, i_rsrc.at[it], i_csrc.at[it], i_r.at[it], i_c.at[it])

    def sums_out(it):
        feat_out(parts_in(it + 1, i_r.at[it], i_c.at[it]), i_f.at[it], "feat", 8 * (it + 1))

    def image_in(it):
        return feat_in(i_f.at[it], "feat", 8 * (it + 1))

    start = jnp.concatenate([start_ref[...], jnp.zeros((NV, PAD - ROWS), F32)], axis=1)
    rows_out(0, start)
    rows_back(0)
    sums_out(0)
    mixed = 0.5 * (start + scale * image_in(0))
    rows_out(1, mixed)
    gram_q_out(0, mixed)
    gram_q_in(0)
    rows_back(1)
    gram_z_in(0)
    sums_out(1)
    mixed = 0.5 * (mixed + scale * image_in(1))
    gram_q_out(1, mixed)
    first_gram = gram_f_in(0)
    gram_q_in(1)
    first_inverse = inverse_factor(first_gram)
    mixed = dot_nn(first_inverse, mixed, HIGHEST)
    gram_z_in(1)
    second_gram = dot_nn(first_inverse, dot_nt(gram_f_in(1), first_inverse, HIGHEST), HIGHEST)
    second_inverse = inverse_factor(second_gram)
    out_ref[...] = dot_nn(second_inverse, mixed, HIGHEST)[:, :ROWS]
    for made, when in pending:
        if when is None:
            made.wait_send()
        else:
            pl.when(when)(made.wait_send)


def per_device(snapshots, spread, start_vectors):
    half_depth = snapshots.shape[1] // HALVES
    vmem = pltpu.VMEM
    shapes = [
        vmem((HOPS + 1, 2, HALVES, PAD, half_depth), BF16),
        vmem((HOPS + 1, 2, HALVES, PAD, half_depth), BF16),
        vmem((9, PAD, WIDE), BF16),
        vmem((3, 3, PAD, WIDE), BF16),
        vmem((2, PAD, WIDE), BF16),
        vmem((2, PAD, WIDE), BF16),
        vmem((2, PAD, WIDE), F32),
        vmem((4, PAD, PAD), BF16),
        vmem((4, PAD, PAD), BF16),
        vmem((8, PAD), F32),
        vmem((2, 8, PAD), F32),
        vmem((2, 8, PAD), F32),
        vmem((2, 8, PAD), F32),
        vmem((2, NV, PAD), BF16),
        vmem((2, 2, NV, PAD), BF16),
        vmem((2, 2, NV, PAD), BF16),
        vmem((2, 2, NV, PAD), BF16),
        vmem((2, 8, PAD), F32),
        vmem((2, 8, PAD), F32),
        vmem((2, 8, PAD), F32),
        vmem((2, 8, PAD), F32),
        vmem((NF, 8, PAD), F32),
        vmem((2, 2, NV, PAD), BF16),
        vmem((2, 2, NV, PAD), BF16),
        vmem((2, 2, NV, PAD), BF16),
        vmem((2, 2, NV, PAD), BF16),
        vmem((2, NF, NV, PAD), BF16),
        vmem((2, Q, NV // 2, 2 * NV), F32),
        vmem((2, NV // 2, 2 * NV), F32),
        vmem((2, 2, NV // 2, 2 * NV), F32),
        vmem((2, NF, NV // 2, 2 * NV), F32),
        pltpu.SemaphoreType.DMA((N_IDS,)),
        pltpu.SemaphoreType.DMA((N_IDS,)),
    ]
    basis = pl.pallas_call(
        kernel,
        out_shape=jax.ShapeDtypeStruct(start_vectors.shape[::-1], F32),
        in_specs=[pl.BlockSpec(memory_space=pltpu.VMEM)] * 3,
        out_specs=pl.BlockSpec(memory_space=pltpu.VMEM),
        scratch_shapes=shapes,
        compiler_params=pltpu.CompilerParams(
            collective_id=0, has_side_effects=True, vmem_limit_bytes=40 * 1024 * 1024
        ),
        cost_estimate=pl.CostEstimate(
            flops=4_000_000_000, bytes_accessed=400_000, transcendentals=200_000
        ),
        name="subspace",
    )(snapshots, spread.reshape(1, -1), start_vectors.T)
    return basis.T


def solution(mesh):
    return jax.shard_map(
        per_device,
        mesh=mesh,
        in_specs=(P("snap", "feat"), P("snap"), P("snap", None)),
        out_specs=P("snap", None),
        check_vma=False,
    )
```

```python
import jax
import jax.numpy as jnp
from jax import lax
from jax.experimental import pallas as pl
from jax.experimental.pallas import tpu as pltpu
from jax.sharding import PartitionSpec as P

Z = 16
Q = 4
NF = 8
NX = 4
HOPS = 4
HALVES = 2
ROWS = 152
PAD = 160
WIDE = 4 * PAD
NARROW = 384
NV = 64
FEATURES = 8192
TOTAL = Z * Q * ROWS
F32 = jnp.float32
BF16 = jnp.bfloat16
HIGHEST = lax.Precision.HIGHEST
R_OFF = (0, 1, 1, 2, 2, 3, 3, 3, 4)
C_OFF = (0, 0, 1, 1, 2, 2, 3, 4, 4)


def dot_nt(a, b, precision=None):
    return lax.dot_general(
        a, b, (((1,), (1,)), ((), ())), precision=precision, preferred_element_type=F32
    )


def dot_nn(a, b, precision=None):
    return lax.dot_general(
        a, b, (((1,), (0,)), ((), ())), precision=precision, preferred_element_type=F32
    )


def eye(n):
    row = lax.broadcasted_iota(jnp.int32, (n, n), 0)
    column = lax.broadcasted_iota(jnp.int32, (n, n), 1)
    return row == column


def column_of(row):
    return jnp.sum(jnp.where(eye(row.shape[1]), row, 0.0), axis=1, keepdims=True)


def row_of(column):
    return jnp.sum(jnp.where(eye(column.shape[0]), column, 0.0), axis=0, keepdims=True)


def inverse_factor(gram):
    n = gram.shape[0]
    on_diagonal = jnp.where(eye(n), gram, 0.0)
    scale_column = lax.rsqrt(jnp.sum(on_diagonal, axis=1, keepdims=True))
    scale_row = lax.rsqrt(jnp.sum(on_diagonal, axis=0, keepdims=True))
    both = jnp.concatenate([gram * scale_column * scale_row, eye(n).astype(F32)], axis=1)
    groups = [both[8 * g : 8 * g + 8] for g in range(n // 8)]
    rows = lax.broadcasted_iota(jnp.int32, (8, 2 * n), 0)
    for j in range(0, n, 2):
        top, r = j // 8, j % 8
        left = {g: jnp.broadcast_to(groups[g][:, j : j + 1], (8, 2 * n)) for g in range(top, n // 8)}
        right = {g: jnp.broadcast_to(groups[g][:, j + 1 : j + 2], (8, 2 * n)) for g in range(top, n // 8)}
        row0, row1 = groups[top][r : r + 1, :], groups[top][r + 1 : r + 2, :]
        a, b, d = left[top][r : r + 1, :], left[top][r + 1 : r + 2, :], right[top][r + 1 : r + 2, :]
        over = 1.0 / (a * d - b * b)
        add0, add1 = (d * row0 - b * row1) * over, (a * row1 - b * row0) * over
        step = b * (1.0 / a) * row0
        for g in range(top, n // 8):
            change = left[g] * add0 + right[g] * add1
            if g == top:
                change = jnp.where(rows > r + 1, change, jnp.where(rows == r + 1, step, 0.0))
            groups[g] = groups[g] - change
    both = jnp.concatenate(groups, axis=0)
    diagonal = jnp.sum(jnp.where(eye(n), both[:, :n], 0.0), axis=1, keepdims=True)
    return both[:, n:] * lax.rsqrt(diagonal) * scale_row


def count_ids():
    sizes = {
        "up": (HOPS + 1) * HALVES,
        "down": (HOPS + 1) * HALVES,
        "across": (HOPS + 1) * HALVES,
        "mate": (HOPS + 1) * HALVES,
        "x": 9,
        "y": 2,
        "gather": 3 * 5,
        "parts": 3 * 4,
        "feat": 3 * 8,
        "gram_q": 2 * 4,
        "gram_z": 2 * 2,
        "gram_f": 2 * 8,
    }
    names, count = {}, 0
    for name, size in sizes.items():
        names[name] = count
        count += size
    return names, count


NAMES, N_IDS = count_ids()


def kernel(
    x_ref,
    spread_ref,
    start_ref,
    out_ref,
    cbuf,
    rbuf,
    pbuf,
    xbuf,
    ysend,
    yrecv,
    keep,
    kq,
    k0,
    width_src,
    width_c,
    width_r,
    width_0,
    w_src,
    w_c,
    w_r,
    w_0,
    d_rsrc,
    d_csrc,
    d_r,
    d_c,
    d_f,
    i_rsrc,
    i_csrc,
    i_r,
    i_c,
    i_f,
    g_q,
    g_zsrc,
    g_z,
    g_f,
    send_sem,
    recv_sem,
):
    snap = lax.axis_index("snap")
    f = lax.axis_index("feat")
    z = snap // Q
    q = snap % Q
    y = q // 2
    c = q % 2
    x = f % NX
    yh = f // NX
    k = f + 1
    is_7 = (k == 7).astype(jnp.int32)
    r_off = (k + 1) // 2 - is_7
    c_off = k // 2 + is_7
    first = f == 0
    not_first = f != 0
    half_depth = cbuf.shape[4]
    upper = z >= Z // 2
    last_rows = (y + upper.astype(jnp.int32)) % 2
    member = q * 2 + yh

    def at(zz, yy, cc, ff):
        return {"snap": ((zz + Z) % Z) * Q + yy * 2 + cc, "feat": ff}

    across = at(z, 1 - y, c, f)
    mate = at(z, y, 1 - c, f)
    pending = []

    def copy(src, dst, name, send, recv, device, when=None):
        made = pltpu.make_async_remote_copy(
            src_ref=src,
            dst_ref=dst,
            send_sem=send_sem.at[NAMES[name] + send],
            recv_sem=recv_sem.at[NAMES[name] + recv],
            device_id=device,
            device_id_type=pl.DeviceIdType.MESH,
        )
        if when is None:
            made.start()
        else:
            pl.when(when)(made.start)
        pending.append((made, when))

    def arrived(dst, name, recv):
        pltpu.make_async_remote_copy(
            src_ref=dst,
            dst_ref=dst,
            send_sem=send_sem.at[NAMES[name]],
            recv_sem=recv_sem.at[NAMES[name] + recv],
            device_id=mate,
            device_id_type=pl.DeviceIdType.MESH,
        ).wait_recv()

    barrier = pltpu.get_barrier_semaphore()
    near = [at(z + 1, y, c, f), at(z - 1, y, c, f), across, mate]
    near += [at(z, y, c, yh * NX + (x + i) % NX) for i in range(1, NX)]
    near += [at(z, y, c, (f + NX) % NF)]
    for device in near:
        pl.semaphore_signal(
            barrier, inc=1, device_id=device, device_id_type=pl.DeviceIdType.MESH
        )
    for half in range(HALVES):
        part = x_ref[:, half * half_depth : (half + 1) * half_depth]
        rest = jnp.zeros((PAD - ROWS, half_depth), BF16)
        cbuf[0, c, half, :ROWS, :] = part
        cbuf[0, c, half, ROWS:, :] = rest
        rbuf[0, y, half, :ROWS, :] = part
        rbuf[0, y, half, ROWS:, :] = rest
    lane = lax.broadcasted_iota(jnp.int32, (1, PAD), 1)
    width_src[...] = jnp.broadcast_to(
        jnp.concatenate(
            [spread_ref[...].astype(F32), jnp.ones((1, PAD - ROWS), F32)], axis=1
        ),
        (8, PAD),
    )
    pl.semaphore_wait(barrier, len(near))

    def send_down(h, half):
        src = rbuf.at[h, y, half]
        if h < HOPS:
            number = (h + 1) * HALVES + half
            copy(src, rbuf.at[h + 1, y, half], "down", number, number, at(z - 1, y, c, f))
        number = h * HALVES + half
        copy(src, rbuf.at[h, y, half], "across", number, number, across, upper if h == HOPS else None)

    def send_up(h, half):
        src = cbuf.at[h, c, half]
        if h < HOPS:
            number = (h + 1) * HALVES + half
            copy(src, cbuf.at[h + 1, c, half], "up", number, number, at(z + 1, y, c, f))
        number = h * HALVES + half
        copy(src, cbuf.at[h, c, half], "mate", number, number, mate)

    def travel(h, halves=range(HALVES)):
        for half in halves:
            number = h * HALVES + half
            if h > 0:
                arrived(rbuf.at[h, y, half], "down", number)
            send_down(h, half)
            if h > 0:
                arrived(cbuf.at[h, c, half], "up", number)
            send_up(h, half)

    def norms(ref, h, i):
        total = jnp.zeros((PAD, half_depth), F32)
        for half in range(HALVES):
            wide = ref[h, i, half].astype(F32)
            total = total + wide * wide
        return jnp.sum(total, axis=1, keepdims=True)

    known = {}

    def c_norms(h):
        if ("c", h) not in known:
            known["c", h] = [norms(cbuf, h, j) for j in range(2)]
        return known["c", h]

    def r_norms(h, picks):
        if ("r", h) not in known:
            known["r", h] = [row_of(norms(rbuf, h, i)) for i in picks]
        return known["r", h]

    def owner_of(kk):
        return (0, 0, 2) if kk == 0 else ((kk - 1) % NX, (kk - 1) // NX, (kk - 1) // NX)

    def tile(ref, kk, *place):
        return ref.at[place + (slice(None), slice(0, NARROW if kk == 8 else WIDE))]

    def make_tile(kk):
        r, h = R_OFF[kk], C_OFF[kk]
        picks = [last_rows] if kk == 8 else [0, 1]
        c_sums, r_sums = c_norms(h), r_norms(r, picks)
        blocks = []
        for j in range(2):
            for n, i in enumerate(picks):
                inner = dot_nt(cbuf[h, j, 0], rbuf[r, i, 0])
                for half in range(1, HALVES):
                    inner = inner + dot_nt(cbuf[h, j, half], rbuf[r, i, half])
                blocks.append(c_sums[j] + r_sums[n] - 2.0 * inner)
        if kk == 8:
            blocks.append(jnp.zeros((PAD, NARROW - 2 * PAD), F32))
        tile(pbuf, kk, kk)[...] = jnp.concatenate(blocks, axis=1).astype(BF16)
        owner, _, slot = owner_of(kk)
        source = (x - owner + NX - 1) % NX % 3
        copy(
            tile(pbuf, kk, kk),
            tile(xbuf, kk, slot, source),
            "x",
            kk,
            slot * 3 + source,
            at(z, y, c, yh * NX + owner),
            x != owner,
        )

    def sum_x(kk):
        owner, last, slot = owner_of(kk)
        kind = 1 if kk == 0 else 0

        @pl.when(x == owner)
        def _():
            for i in range(3):
                arrived(tile(xbuf, kk, slot, i), "x", slot * 3 + i)
            total = tile(pbuf, kk, kk)[...].astype(F32)
            for i in range(3):
                total = total + tile(xbuf, kk, slot, i)[...].astype(F32)

            @pl.when(yh == last)
            def _():
                tile(keep, kk, kind)[...] = total

            @pl.when(yh != last)
            def _():
                tile(ysend, kk, kind)[...] = total.astype(BF16)

        copy(
            tile(ysend, kk, kind),
            tile(yrecv, kk, kind),
            "y",
            kind,
            kind,
            at(z, y, c, (f + NX) % NF),
            (x == owner) & (yh != last),
        )

    def rows_in(h):
        for half in range(HALVES):
            arrived(rbuf.at[h, 1 - y, half], "across", h * HALVES + half)

    def columns_in(h):
        for half in range(HALVES):
            arrived(cbuf.at[h, 1 - c, half], "mate", h * HALVES + half)

    def spread_out(src, c_dst, r_dst, z_dst, base):
        for i in range(2):
            copy(src, r_dst.at[y], "gather", base + i, base + y, at(z - r_off, i, c, f))
        for i in range(2):
            number = base + 2 + i
            copy(src, c_dst.at[c], "gather", number, base + 2 + c, at(z + c_off, y, i, f), not_first)

        copy(src, c_dst.at[c], "gather", base + 2, base + 2 + c, mate, first)
        copy(src, z_dst.at[y], "gather", base + 4, base + 4, across, first)

        @pl.when(first)
        def _():
            c_dst[c] = src[...]
            z_dst[y] = src[...]

    def spread_in(c_dst, r_dst, z_dst, base):
        for i in range(2):
            arrived(r_dst.at[i], "gather", base + i)

        @pl.when(not_first)
        def _():
            for i in range(2):
                arrived(c_dst.at[i], "gather", base + 2 + i)

        @pl.when(first)
        def _():
            arrived(c_dst.at[1 - c], "gather", base + 2 + 1 - c)
            arrived(z_dst.at[1 - y], "gather", base + 4)

    travel(0)
    travel(1)
    columns_in(0)
    rows_in(0)
    make_tile(0)
    travel(2)
    rows_in(1)
    make_tile(1)
    columns_in(1)
    make_tile(2)
    travel(3)
    sum_x(0)
    rows_in(2)
    make_tile(3)
    columns_in(2)
    make_tile(4)
    travel(4, range(HALVES // 2))
    sum_x(1)
    sum_x(2)
    rows_in(3)
    make_tile(5)
    columns_in(3)
    make_tile(6)
    travel(4, range(HALVES // 2, HALVES))
    sum_x(3)
    sum_x(4)
    columns_in(4)
    make_tile(7)
    pl.when(upper)(lambda: rows_in(4))
    make_tile(8)
    spread_out(width_src, width_c, width_r, width_0, 0)
    sum_x(5)
    sum_x(6)
    spread_in(width_c, width_r, width_0, 0)
    sum_x(7)
    sum_x(8)

    def kernel_block(kind, b, c_column, r_row, dst, place):
        row = lax.broadcasted_iota(jnp.int32, (PAD, PAD), 0)
        column = lax.broadcasted_iota(jnp.int32, (PAD, PAD), 1)
        inside = (row < ROWS) & (column < ROWS)
        lanes = slice(b * PAD, (b + 1) * PAD)
        distance = keep[kind, :, lanes] + yrecv[kind, :, lanes].astype(F32)
        exponent = -(distance / (c_column * r_row)) / FEATURES
        dst[place] = jnp.where(inside, jnp.exp(exponent), 0.0).astype(BF16)

    c_columns = [column_of(width_c[j, :1, :]) for j in range(2)]

    @pl.when(first)
    def _():
        arrived(yrecv.at[1], "y", 1)
        for b in range(4):
            kernel_block(1, b, c_columns[b // 2], width_0[b % 2, :1, :], k0, b)

    @pl.when(f != NF - 1)
    def _():
        arrived(yrecv.at[0], "y", 0)
        for b in range(4):
            kernel_block(0, b, c_columns[b // 2], width_r[b % 2, :1, :], kq, b)

    @pl.when(f == NF - 1)
    def _():
        arrived(tile(yrecv, 8, 0), "y", 0)
        for j in range(2):
            kq[2 * j + 1 - last_rows] = jnp.zeros((PAD, PAD), BF16)
            kernel_block(0, j, c_columns[j], width_r[last_rows, :1, :], kq, 2 * j + last_rows)

    def parts_out(index, height, w_of, r_src, c_src, got_r, got_c):
        base = index * 4
        kind = got_r.dtype
        for i in range(2):
            part = dot_nn(w_of("c", 0), kq[i]) + dot_nn(w_of("c", 1), kq[2 + i])
            r_src[i] = part[:height].astype(kind)
            copy(r_src.at[i], got_r.at[y], "parts", base + i, base + y, at(z + r_off, i, c, f))
        for j in range(2):
            part = dot_nt(w_of("r", 0), kq[2 * j]) + dot_nt(w_of("r", 1), kq[2 * j + 1])

            @pl.when(not_first)
            def _(part=part, j=j):
                c_src[j] = part[:height].astype(kind)

            @pl.when(first)
            def _(part=part, j=j):
                own = part + dot_nt(w_of("0", 0), k0[2 * j]) + dot_nt(w_of("0", 1), k0[2 * j + 1])
                c_src[j] = own[:height].astype(kind)

            copy(c_src.at[j], got_c.at[c], "parts", base + 2 + j, base + 2 + c, at(z - c_off, y, j, f), not_first)
        copy(c_src.at[1 - c], got_c.at[c], "parts", base + 2, base + 2 + c, mate, first)

        @pl.when(first)
        def _():
            got_c[c] = c_src[c]

    def parts_in(index, got_r, got_c):
        base = index * 4
        for i in range(2):
            arrived(got_r.at[i], "parts", base + i)

        @pl.when(not_first)
        def _():
            for i in range(2):
                arrived(got_c.at[i], "parts", base + 2 + i)

        pl.when(first)(lambda: arrived(got_c.at[1 - c], "parts", base + 2 + 1 - c))
        total = got_r[0].astype(F32) + got_r[1].astype(F32)
        return total + got_c[0].astype(F32) + got_c[1].astype(F32)

    def feat_out(total, got_f, name, base):
        got_f[f] = total.astype(got_f.dtype)
        for i in range(1, NF):
            copy(got_f.at[f], got_f.at[f], name, base + i, base + i, at(z, y, c, (f + i) % NF))

    def feat_in(got_f, name, base):
        for i in range(1, NF):
            arrived(got_f.at[(f + NF - i) % NF], name, base + i)
        total = got_f[0].astype(F32)
        for i in range(1, NF):
            total = total + got_f[i].astype(F32)
        return total

    def gram_q_out(it, mixed):
        gram = dot_nt(mixed, mixed, HIGHEST)
        g_q[it, q] = jnp.concatenate([gram[: NV // 2], gram[NV // 2 :]], axis=1)
        for i in range(1, Q):
            there = (q + i) % Q
            copy(g_q.at[it, q], g_q.at[it, q], "gram_q", 4 * it + i, 4 * it + i, at(z, there // 2, there % 2, f))

    def gram_q_in(it):
        for i in range(1, Q):
            arrived(g_q.at[it, (q + Q - i) % Q], "gram_q", 4 * it + i)
        here = g_q[it, 0]
        for i in range(1, Q):
            here = here + g_q[it, i]
        g_zsrc[it] = here

        @pl.when(member == 0)
        def _():
            g_z[it, 0] = here

        base = 2 * it
        there = at(z - member, y, c, f)
        copy(g_zsrc.at[it], g_z.at[it, 0], "gram_z", base, base, there, member != 0)
        there = at(z + 8 - member, y, c, f)
        copy(g_zsrc.at[it], g_z.at[it, 1], "gram_z", base + 1, base + 1, there)

    def gram_z_in(it):
        pl.when(member != 0)(lambda: arrived(g_z.at[it, 0], "gram_z", 2 * it))
        arrived(g_z.at[it, 1], "gram_z", 2 * it + 1)
        g_f[it, member] = g_z[it, 0] + g_z[it, 1]
        mine = g_f.at[it, member]
        for i in range(1, 8):
            there = (member + i) % 8
            device = at(z, there // 4, there // 2 % 2, there % 2 * NX + x)
            copy(mine, mine, "gram_f", 8 * it + i, 8 * it + i, device)

    def gram_f_in(it):
        for i in range(1, 8):
            arrived(g_f.at[it, (member + 8 - i) % 8], "gram_f", 8 * it + i)
        pair = g_f[it, 0]
        for i in range(1, 8):
            pair = pair + g_f[it, i]
        pair = pair / TOTAL
        return jnp.concatenate([pair[:, :NV], pair[:, NV:]], axis=0)

    ones = jnp.ones((16, PAD), BF16)
    parts_out(0, 8, lambda kind, i: ones, d_rsrc, d_csrc, d_r, d_c)
    feat_out(parts_in(0, d_r, d_c), d_f, "feat", 0)
    degree = feat_in(d_f, "feat", 0)[:1]
    scale = jnp.where(lane < ROWS, 1.0 / jnp.sqrt(jnp.where(lane < ROWS, degree, 1.0)), 0.0)

    def rows_out(it, vectors):
        w_src[it] = (scale * vectors).astype(BF16)
        spread_out(w_src.at[it], w_c.at[it], w_r.at[it], w_0.at[it], 5 * (it + 1))

    def rows_back(it):
        spread_in(w_c.at[it], w_r.at[it], w_0.at[it], 5 * (it + 1))

        def w_of(kind, i):
            return {"c": w_c, "r": w_r, "0": w_0}[kind][it, i]

        parts_out(it + 1, NV, w_of, i_rsrc.at[it], i_csrc.at[it], i_r.at[it], i_c.at[it])

    def sums_out(it):
        feat_out(parts_in(it + 1, i_r.at[it], i_c.at[it]), i_f.at[it], "feat", 8 * (it + 1))

    def image_in(it):
        return feat_in(i_f.at[it], "feat", 8 * (it + 1))

    start = jnp.concatenate([start_ref[...], jnp.zeros((NV, PAD - ROWS), F32)], axis=1)
    rows_out(0, start)
    rows_back(0)
    sums_out(0)
    mixed = 0.5 * (start + scale * image_in(0))
    rows_out(1, mixed)
    gram_q_out(0, mixed)
    gram_q_in(0)
    rows_back(1)
    sums_out(1)
    gram_z_in(0)
    mixed = 0.5 * (mixed + scale * image_in(1))
    gram_q_out(1, mixed)
    gram_q_in(1)
    first_inverse = inverse_factor(gram_f_in(0))
    mixed = dot_nn(first_inverse, mixed, HIGHEST)
    gram_z_in(1)
    second_gram = dot_nn(first_inverse, dot_nt(gram_f_in(1), first_inverse, HIGHEST), HIGHEST)
    second_inverse = inverse_factor(second_gram)
    out_ref[...] = dot_nn(second_inverse, mixed, HIGHEST)[:, :ROWS]
    for made, when in pending:
        if when is None:
            made.wait_send()
        else:
            pl.when(when)(made.wait_send)


def per_device(snapshots, spread, start_vectors):
    half_depth = snapshots.shape[1] // HALVES
    vmem = pltpu.VMEM
    shapes = [
        vmem((HOPS + 1, 2, HALVES, PAD, half_depth), BF16),
        vmem((HOPS + 1, 2, HALVES, PAD, half_depth), BF16),
        vmem((9, PAD, WIDE), BF16),
        vmem((3, 3, PAD, WIDE), BF16),
        vmem((2, PAD, WIDE), BF16),
        vmem((2, PAD, WIDE), BF16),
        vmem((2, PAD, WIDE), F32),
        vmem((4, PAD, PAD), BF16),
        vmem((4, PAD, PAD), BF16),
        vmem((8, PAD), F32),
        vmem((2, 8, PAD), F32),
        vmem((2, 8, PAD), F32),
        vmem((2, 8, PAD), F32),
        vmem((2, NV, PAD), BF16),
        vmem((2, 2, NV, PAD), BF16),
        vmem((2, 2, NV, PAD), BF16),
        vmem((2, 2, NV, PAD), BF16),
        vmem((2, 8, PAD), F32),
        vmem((2, 8, PAD), F32),
        vmem((2, 8, PAD), F32),
        vmem((2, 8, PAD), F32),
        vmem((NF, 8, PAD), F32),
        vmem((2, 2, NV, PAD), BF16),
        vmem((2, 2, NV, PAD), BF16),
        vmem((2, 2, NV, PAD), BF16),
        vmem((2, 2, NV, PAD), BF16),
        vmem((2, NF, NV, PAD), BF16),
        vmem((2, Q, NV // 2, 2 * NV), F32),
        vmem((2, NV // 2, 2 * NV), F32),
        vmem((2, 2, NV // 2, 2 * NV), F32),
        vmem((2, NF, NV // 2, 2 * NV), F32),
        pltpu.SemaphoreType.DMA((N_IDS,)),
        pltpu.SemaphoreType.DMA((N_IDS,)),
    ]
    basis = pl.pallas_call(
        kernel,
        out_shape=jax.ShapeDtypeStruct(start_vectors.shape[::-1], F32),
        in_specs=[pl.BlockSpec(memory_space=pltpu.VMEM)] * 3,
        out_specs=pl.BlockSpec(memory_space=pltpu.VMEM),
        scratch_shapes=shapes,
        compiler_params=pltpu.CompilerParams(
            collective_id=0, has_side_effects=True, vmem_limit_bytes=40 * 1024 * 1024
        ),
        cost_estimate=pl.CostEstimate(
            flops=4_000_000_000, bytes_accessed=400_000, transcendentals=200_000
        ),
        name="subspace",
    )(snapshots, spread.reshape(1, -1), start_vectors.T)
    return basis.T


def solution(mesh):
    return jax.shard_map(
        per_device,
        mesh=mesh,
        in_specs=(P("snap", "feat"), P("snap"), P("snap", None)),
        out_specs=P("snap", None),
        check_vma=False,
    )
```

```python
import jax
import jax.numpy as jnp
from jax import lax
from jax.experimental import pallas as pl
from jax.experimental.pallas import tpu as pltpu
from jax.sharding import PartitionSpec as P

Z = 16
Q = 4
NF = 8
NX = 4
HOPS = 4
HALVES = 2
ROWS = 152
PAD = 160
WIDE = 4 * PAD
NARROW = 384
NV = 64
FEATURES = 8192
TOTAL = Z * Q * ROWS
F32 = jnp.float32
BF16 = jnp.bfloat16
HIGHEST = lax.Precision.HIGHEST
R_OFF = (0, 1, 1, 2, 2, 3, 3, 3, 4)
C_OFF = (0, 0, 1, 1, 2, 2, 3, 4, 4)


def dot_nt(a, b, precision=None):
    return lax.dot_general(
        a, b, (((1,), (1,)), ((), ())), precision=precision, preferred_element_type=F32
    )


def dot_nn(a, b, precision=None):
    return lax.dot_general(
        a, b, (((1,), (0,)), ((), ())), precision=precision, preferred_element_type=F32
    )


def eye(n):
    row = lax.broadcasted_iota(jnp.int32, (n, n), 0)
    column = lax.broadcasted_iota(jnp.int32, (n, n), 1)
    return row == column


def column_of(row):
    return jnp.sum(jnp.where(eye(row.shape[1]), row, 0.0), axis=1, keepdims=True)


def row_of(column):
    return jnp.sum(jnp.where(eye(column.shape[0]), column, 0.0), axis=0, keepdims=True)


def inverse_factor(gram):
    n = gram.shape[0]
    on_diagonal = jnp.where(eye(n), gram, 0.0)
    scale_column = lax.rsqrt(jnp.sum(on_diagonal, axis=1, keepdims=True))
    scale_row = lax.rsqrt(jnp.sum(on_diagonal, axis=0, keepdims=True))
    both = jnp.concatenate([gram * scale_column * scale_row, eye(n).astype(F32)], axis=1)
    groups = [both[8 * g : 8 * g + 8] for g in range(n // 8)]
    rows = lax.broadcasted_iota(jnp.int32, (8, 2 * n), 0)
    for j in range(0, n, 2):
        top, r = j // 8, j % 8
        left = {g: jnp.broadcast_to(groups[g][:, j : j + 1], (8, 2 * n)) for g in range(top, n // 8)}
        right = {g: jnp.broadcast_to(groups[g][:, j + 1 : j + 2], (8, 2 * n)) for g in range(top, n // 8)}
        row0, row1 = groups[top][r : r + 1, :], groups[top][r + 1 : r + 2, :]
        a, b, d = left[top][r : r + 1, :], left[top][r + 1 : r + 2, :], right[top][r + 1 : r + 2, :]
        over = 1.0 / (a * d - b * b)
        add0, add1 = (d * row0 - b * row1) * over, (a * row1 - b * row0) * over
        step = b * (1.0 / a) * row0
        for g in range(top, n // 8):
            change = left[g] * add0 + right[g] * add1
            if g == top:
                change = jnp.where(rows > r + 1, change, jnp.where(rows == r + 1, step, 0.0))
            groups[g] = groups[g] - change
    both = jnp.concatenate(groups, axis=0)
    diagonal = jnp.sum(jnp.where(eye(n), both[:, :n], 0.0), axis=1, keepdims=True)
    return both[:, n:] * lax.rsqrt(diagonal) * scale_row


def count_ids():
    sizes = {
        "up": (HOPS + 1) * HALVES,
        "down": (HOPS + 1) * HALVES,
        "across": (HOPS + 1) * HALVES,
        "mate": (HOPS + 1) * HALVES,
        "x": 9,
        "y": 2,
        "gather": 3 * 5,
        "parts": 3 * 4,
        "feat": 3 * 8,
        "gram_q": 2 * 4,
        "gram_z": 2 * 2,
        "gram_f": 2 * 8,
    }
    names, count = {}, 0
    for name, size in sizes.items():
        names[name] = count
        count += size
    return names, count


NAMES, N_IDS = count_ids()


def kernel(
    x_ref,
    spread_ref,
    start_ref,
    out_ref,
    cbuf,
    rbuf,
    pbuf,
    xbuf,
    ysend,
    yrecv,
    keep,
    kq,
    k0,
    width_src,
    width_c,
    width_r,
    width_0,
    w_src,
    w_c,
    w_r,
    w_0,
    d_rsrc,
    d_csrc,
    d_r,
    d_c,
    d_f,
    i_rsrc,
    i_csrc,
    i_r,
    i_c,
    i_f,
    g_q,
    g_zsrc,
    g_z,
    g_f,
    send_sem,
    recv_sem,
):
    snap = lax.axis_index("snap")
    f = lax.axis_index("feat")
    z = snap // Q
    q = snap % Q
    y = q // 2
    c = q % 2
    x = f % NX
    yh = f // NX

    def tile_of(core):
        k = f + 1 if core == 0 else NF - f
        is_7 = (k == 7).astype(jnp.int32)
        return k, (k + 1) // 2 - is_7, k // 2 + is_7

    (k_a, r_off_a, c_off_a), (k_b, r_off_b, c_off_b) = tile_of(0), tile_of(1)
    c_offs = [c_off_a, c_off_b]
    k = k_a + c * (k_b - k_a)
    r_off = r_off_a + c * (r_off_b - r_off_a)
    c_off = c_off_a + c * (c_off_b - c_off_a)
    first = k == 1
    not_first = k != 1
    is_last = k == NF
    from_away = [not_first | (c != i) for i in range(2)]
    half_depth = cbuf.shape[4]
    upper = z >= Z // 2
    last_rows = (y + upper.astype(jnp.int32)) % 2
    member = q * 2 + yh

    def at(zz, yy, cc, ff):
        return {"snap": ((zz + Z) % Z) * Q + yy * 2 + cc, "feat": ff}

    across = at(z, 1 - y, c, f)
    mate = at(z, y, 1 - c, f)
    pending = []

    def copy(src, dst, name, send, recv, device, when=None):
        made = pltpu.make_async_remote_copy(
            src_ref=src,
            dst_ref=dst,
            send_sem=send_sem.at[NAMES[name] + send],
            recv_sem=recv_sem.at[NAMES[name] + recv],
            device_id=device,
            device_id_type=pl.DeviceIdType.MESH,
        )
        if when is None:
            made.start()
        else:
            pl.when(when)(made.start)
        pending.append((made, when))

    def arrived(dst, name, recv):
        pltpu.make_async_remote_copy(
            src_ref=dst,
            dst_ref=dst,
            send_sem=send_sem.at[NAMES[name]],
            recv_sem=recv_sem.at[NAMES[name] + recv],
            device_id=mate,
            device_id_type=pl.DeviceIdType.MESH,
        ).wait_recv()

    barrier = pltpu.get_barrier_semaphore()
    near = [at(z + 1, y, c, f), at(z - 1, y, c, f), across, mate]
    near += [at(z, y, c, yh * NX + (x + i) % NX) for i in range(1, NX)]
    near += [at(z, y, c, (f + NX) % NF)]
    for device in near:
        pl.semaphore_signal(
            barrier, inc=1, device_id=device, device_id_type=pl.DeviceIdType.MESH
        )
    for half in range(HALVES):
        part = x_ref[:, half * half_depth : (half + 1) * half_depth]
        rest = jnp.zeros((PAD - ROWS, half_depth), BF16)
        cbuf[0, c, half, :ROWS, :] = part
        cbuf[0, c, half, ROWS:, :] = rest
        rbuf[0, y, half, :ROWS, :] = part
        rbuf[0, y, half, ROWS:, :] = rest
    lane = lax.broadcasted_iota(jnp.int32, (1, PAD), 1)
    width_src[...] = jnp.broadcast_to(
        jnp.concatenate(
            [spread_ref[...].astype(F32), jnp.ones((1, PAD - ROWS), F32)], axis=1
        ),
        (8, PAD),
    )
    pl.semaphore_wait(barrier, len(near))

    def send_down(h, half):
        src = rbuf.at[h, y, half]
        if h < HOPS:
            number = (h + 1) * HALVES + half
            copy(src, rbuf.at[h + 1, y, half], "down", number, number, at(z - 1, y, c, f))
        number = h * HALVES + half
        copy(src, rbuf.at[h, y, half], "across", number, number, across, upper if h == HOPS else None)

    def send_up(h, half):
        src = cbuf.at[h, c, half]
        if h < HOPS:
            number = (h + 1) * HALVES + half
            copy(src, cbuf.at[h + 1, c, half], "up", number, number, at(z + 1, y, c, f))
        number = h * HALVES + half
        copy(src, cbuf.at[h, c, half], "mate", number, number, mate)

    def travel(h, halves=range(HALVES)):
        for half in halves:
            number = h * HALVES + half
            if h > 0:
                arrived(rbuf.at[h, y, half], "down", number)
            send_down(h, half)
            if h > 0:
                arrived(cbuf.at[h, c, half], "up", number)
            send_up(h, half)

    def norms(ref, h, i):
        total = jnp.zeros((PAD, half_depth), F32)
        for half in range(HALVES):
            wide = ref[h, i, half].astype(F32)
            total = total + wide * wide
        return jnp.sum(total, axis=1, keepdims=True)

    known = {}

    def c_norms(h):
        if ("c", h) not in known:
            known["c", h] = [norms(cbuf, h, j) for j in range(2)]
        return known["c", h]

    def r_norms(h, picks):
        if ("r", h) not in known:
            known["r", h] = [row_of(norms(rbuf, h, i)) for i in picks]
        return known["r", h]

    def owner_of(kk):
        place, last = (0, 0) if kk == 0 else ((kk - 1) % NX, (kk - 1) // NX)
        owner = place + c * (NX - 1 - 2 * place)
        return owner, last + c * (1 - 2 * last), 2 if kk == 0 else last

    def tile(ref, kk, *place):
        return ref.at[place + (slice(None), slice(0, NARROW if kk == 8 else WIDE))]

    def make_tile(kk):
        r, h = R_OFF[kk], C_OFF[kk]
        picks = [last_rows] if kk == 8 else [0, 1]
        c_sums, r_sums = c_norms(h), r_norms(r, picks)
        blocks = []
        for j in range(2):
            for n, i in enumerate(picks):
                inner = dot_nt(cbuf[h, j, 0], rbuf[r, i, 0])
                for half in range(1, HALVES):
                    inner = inner + dot_nt(cbuf[h, j, half], rbuf[r, i, half])
                blocks.append(c_sums[j] + r_sums[n] - 2.0 * inner)
        if kk == 8:
            blocks.append(jnp.zeros((PAD, NARROW - 2 * PAD), F32))
        tile(pbuf, kk, kk)[...] = jnp.concatenate(blocks, axis=1).astype(BF16)
        owner, _, slot = owner_of(kk)
        source = (x - owner + NX - 1) % NX % 3
        copy(
            tile(pbuf, kk, kk),
            tile(xbuf, kk, slot, source),
            "x",
            kk,
            slot * 3 + source,
            at(z, y, c, yh * NX + owner),
            x != owner,
        )

    def sum_x(kk):
        owner, last, slot = owner_of(kk)
        kind = 1 if kk == 0 else 0

        @pl.when(x == owner)
        def _():
            for i in range(3):
                arrived(tile(xbuf, kk, slot, i), "x", slot * 3 + i)
            total = tile(pbuf, kk, kk)[...].astype(F32)
            for i in range(3):
                total = total + tile(xbuf, kk, slot, i)[...].astype(F32)

            @pl.when(yh == last)
            def _():
                tile(keep, kk, kind)[...] = total

            @pl.when(yh != last)
            def _():
                tile(ysend, kk, kind)[...] = total.astype(BF16)

        copy(
            tile(ysend, kk, kind),
            tile(yrecv, kk, kind),
            "y",
            kind,
            kind,
            at(z, y, c, (f + NX) % NF),
            (x == owner) & (yh != last),
        )

    def rows_in(h):
        for half in range(HALVES):
            arrived(rbuf.at[h, 1 - y, half], "across", h * HALVES + half)

    def columns_in(h):
        for half in range(HALVES):
            arrived(cbuf.at[h, 1 - c, half], "mate", h * HALVES + half)

    def spread_out(src, c_dst, r_dst, z_dst, base):
        for i in range(2):
            copy(src, r_dst.at[y], "gather", base + i, base + y, at(z - r_off, i, c, f))
        for i in range(2):
            there = at(z + c_offs[i], y, i, f)
            copy(src, c_dst.at[c], "gather", base + 2 + i, base + 2 + c, there, from_away[i])
        copy(src, z_dst.at[y], "gather", base + 4, base + 4, across, first)

        @pl.when(first)
        def _():
            c_dst[c] = src[...]
            z_dst[y] = src[...]

    def spread_in(c_dst, r_dst, z_dst, base):
        for i in range(2):
            arrived(r_dst.at[i], "gather", base + i)
        for i in range(2):
            pl.when(from_away[i])(lambda i=i: arrived(c_dst.at[i], "gather", base + 2 + i))
        pl.when(first)(lambda: arrived(z_dst.at[1 - y], "gather", base + 4))

    travel(0)
    travel(1)
    columns_in(0)
    rows_in(0)
    make_tile(0)
    travel(2)
    rows_in(1)
    make_tile(1)
    columns_in(1)
    make_tile(2)
    travel(3)
    sum_x(0)
    rows_in(2)
    make_tile(3)
    columns_in(2)
    make_tile(4)
    travel(4, range(HALVES // 2))
    sum_x(1)
    sum_x(2)
    rows_in(3)
    make_tile(5)
    columns_in(3)
    make_tile(6)
    travel(4, range(HALVES // 2, HALVES))
    sum_x(3)
    sum_x(4)
    columns_in(4)
    make_tile(7)
    pl.when(upper)(lambda: rows_in(4))
    make_tile(8)
    spread_out(width_src, width_c, width_r, width_0, 0)
    sum_x(5)
    sum_x(6)
    spread_in(width_c, width_r, width_0, 0)
    sum_x(7)
    sum_x(8)

    def kernel_block(kind, b, c_column, r_row, dst, place):
        row = lax.broadcasted_iota(jnp.int32, (PAD, PAD), 0)
        column = lax.broadcasted_iota(jnp.int32, (PAD, PAD), 1)
        inside = (row < ROWS) & (column < ROWS)
        lanes = slice(b * PAD, (b + 1) * PAD)
        distance = keep[kind, :, lanes] + yrecv[kind, :, lanes].astype(F32)
        exponent = -(distance / (c_column * r_row)) / FEATURES
        dst[place] = jnp.where(inside, jnp.exp(exponent), 0.0).astype(BF16)

    c_columns = [column_of(width_c[j, :1, :]) for j in range(2)]

    @pl.when(first)
    def _():
        arrived(yrecv.at[1], "y", 1)
        for b in range(4):
            kernel_block(1, b, c_columns[b // 2], width_0[b % 2, :1, :], k0, b)

    @pl.when(jnp.logical_not(is_last))
    def _():
        arrived(yrecv.at[0], "y", 0)
        for b in range(4):
            kernel_block(0, b, c_columns[b // 2], width_r[b % 2, :1, :], kq, b)

    @pl.when(is_last)
    def _():
        arrived(tile(yrecv, 8, 0), "y", 0)
        for j in range(2):
            kq[2 * j + 1 - last_rows] = jnp.zeros((PAD, PAD), BF16)
            kernel_block(0, j, c_columns[j], width_r[last_rows, :1, :], kq, 2 * j + last_rows)

    def parts_out(index, height, w_of, r_src, c_src, got_r, got_c):
        base = index * 4
        kind = got_r.dtype
        for i in range(2):
            part = dot_nn(w_of("c", 0), kq[i]) + dot_nn(w_of("c", 1), kq[2 + i])
            r_src[i] = part[:height].astype(kind)
            copy(r_src.at[i], got_r.at[y], "parts", base + i, base + y, at(z + r_off, i, c, f))
        for j in range(2):
            part = dot_nt(w_of("r", 0), kq[2 * j]) + dot_nt(w_of("r", 1), kq[2 * j + 1])

            @pl.when(not_first)
            def _(part=part, j=j):
                c_src[j] = part[:height].astype(kind)

            @pl.when(first)
            def _(part=part, j=j):
                own = part + dot_nt(w_of("0", 0), k0[2 * j]) + dot_nt(w_of("0", 1), k0[2 * j + 1])
                c_src[j] = own[:height].astype(kind)

            there = at(z - c_off, y, j, f)
            copy(c_src.at[j], got_c.at[c], "parts", base + 2 + j, base + 2 + c, there, from_away[j])

        @pl.when(first)
        def _():
            got_c[c] = c_src[c]

    def parts_in(index, got_r, got_c):
        base = index * 4
        for i in range(2):
            arrived(got_r.at[i], "parts", base + i)

        for i in range(2):
            pl.when(from_away[i])(lambda i=i: arrived(got_c.at[i], "parts", base + 2 + i))
        total = got_r[0].astype(F32) + got_r[1].astype(F32)
        return total + got_c[0].astype(F32) + got_c[1].astype(F32)

    def feat_out(total, got_f, name, base):
        got_f[f] = total.astype(got_f.dtype)
        for i in range(1, NF):
            copy(got_f.at[f], got_f.at[f], name, base + i, base + i, at(z, y, c, (f + i) % NF))

    def feat_in(got_f, name, base):
        for i in range(1, NF):
            arrived(got_f.at[(f + NF - i) % NF], name, base + i)
        total = got_f[0].astype(F32)
        for i in range(1, NF):
            total = total + got_f[i].astype(F32)
        return total

    def gram_q_out(it, mixed):
        gram = dot_nt(mixed, mixed, HIGHEST)
        g_q[it, q] = jnp.concatenate([gram[: NV // 2], gram[NV // 2 :]], axis=1)
        for i in range(1, Q):
            there = (q + i) % Q
            copy(g_q.at[it, q], g_q.at[it, q], "gram_q", 4 * it + i, 4 * it + i, at(z, there // 2, there % 2, f))

    def gram_q_in(it):
        for i in range(1, Q):
            arrived(g_q.at[it, (q + Q - i) % Q], "gram_q", 4 * it + i)
        here = g_q[it, 0]
        for i in range(1, Q):
            here = here + g_q[it, i]
        g_zsrc[it] = here

        @pl.when(member == 0)
        def _():
            g_z[it, 0] = here

        base = 2 * it
        there = at(z - member, y, c, f)
        copy(g_zsrc.at[it], g_z.at[it, 0], "gram_z", base, base, there, member != 0)
        there = at(z + 8 - member, y, c, f)
        copy(g_zsrc.at[it], g_z.at[it, 1], "gram_z", base + 1, base + 1, there)

    def gram_z_in(it):
        pl.when(member != 0)(lambda: arrived(g_z.at[it, 0], "gram_z", 2 * it))
        arrived(g_z.at[it, 1], "gram_z", 2 * it + 1)
        g_f[it, member] = g_z[it, 0] + g_z[it, 1]
        mine = g_f.at[it, member]
        for i in range(1, 8):
            there = (member + i) % 8
            device = at(z, there // 4, there // 2 % 2, there % 2 * NX + x)
            copy(mine, mine, "gram_f", 8 * it + i, 8 * it + i, device)

    def gram_f_in(it):
        for i in range(1, 8):
            arrived(g_f.at[it, (member + 8 - i) % 8], "gram_f", 8 * it + i)
        pair = g_f[it, 0]
        for i in range(1, 8):
            pair = pair + g_f[it, i]
        pair = pair / TOTAL
        return jnp.concatenate([pair[:, :NV], pair[:, NV:]], axis=0)

    ones = jnp.ones((16, PAD), BF16)
    parts_out(0, 8, lambda kind, i: ones, d_rsrc, d_csrc, d_r, d_c)
    feat_out(parts_in(0, d_r, d_c), d_f, "feat", 0)
    degree = feat_in(d_f, "feat", 0)[:1]
    scale = jnp.where(lane < ROWS, 1.0 / jnp.sqrt(jnp.where(lane < ROWS, degree, 1.0)), 0.0)

    def rows_out(it, vectors):
        w_src[it] = (scale * vectors).astype(BF16)
        spread_out(w_src.at[it], w_c.at[it], w_r.at[it], w_0.at[it], 5 * (it + 1))

    def rows_back(it):
        spread_in(w_c.at[it], w_r.at[it], w_0.at[it], 5 * (it + 1))

        def w_of(kind, i):
            return {"c": w_c, "r": w_r, "0": w_0}[kind][it, i]

        parts_out(it + 1, NV, w_of, i_rsrc.at[it], i_csrc.at[it], i_r.at[it], i_c.at[it])

    def sums_out(it):
        feat_out(parts_in(it + 1, i_r.at[it], i_c.at[it]), i_f.at[it], "feat", 8 * (it + 1))

    def image_in(it):
        return feat_in(i_f.at[it], "feat", 8 * (it + 1))

    start = jnp.concatenate([start_ref[...], jnp.zeros((NV, PAD - ROWS), F32)], axis=1)
    rows_out(0, start)
    rows_back(0)
    sums_out(0)
    mixed = 0.5 * (start + scale * image_in(0))
    rows_out(1, mixed)
    gram_q_out(0, mixed)
    gram_q_in(0)
    rows_back(1)
    sums_out(1)
    gram_z_in(0)
    mixed = 0.5 * (mixed + scale * image_in(1))
    gram_q_out(1, mixed)
    gram_q_in(1)
    first_inverse = inverse_factor(gram_f_in(0))
    mixed = dot_nn(first_inverse, mixed, HIGHEST)
    gram_z_in(1)
    second_gram = dot_nn(first_inverse, dot_nt(gram_f_in(1), first_inverse, HIGHEST), HIGHEST)
    second_inverse = inverse_factor(second_gram)
    out_ref[...] = dot_nn(second_inverse, mixed, HIGHEST)[:, :ROWS]
    for made, when in pending:
        if when is None:
            made.wait_send()
        else:
            pl.when(when)(made.wait_send)


def per_device(snapshots, spread, start_vectors):
    half_depth = snapshots.shape[1] // HALVES
    vmem = pltpu.VMEM
    shapes = [
        vmem((HOPS + 1, 2, HALVES, PAD, half_depth), BF16),
        vmem((HOPS + 1, 2, HALVES, PAD, half_depth), BF16),
        vmem((9, PAD, WIDE), BF16),
        vmem((3, 3, PAD, WIDE), BF16),
        vmem((2, PAD, WIDE), BF16),
        vmem((2, PAD, WIDE), BF16),
        vmem((2, PAD, WIDE), F32),
        vmem((4, PAD, PAD), BF16),
        vmem((4, PAD, PAD), BF16),
        vmem((8, PAD), F32),
        vmem((2, 8, PAD), F32),
        vmem((2, 8, PAD), F32),
        vmem((2, 8, PAD), F32),
        vmem((2, NV, PAD), BF16),
        vmem((2, 2, NV, PAD), BF16),
        vmem((2, 2, NV, PAD), BF16),
        vmem((2, 2, NV, PAD), BF16),
        vmem((2, 8, PAD), F32),
        vmem((2, 8, PAD), F32),
        vmem((2, 8, PAD), F32),
        vmem((2, 8, PAD), F32),
        vmem((NF, 8, PAD), F32),
        vmem((2, 2, NV, PAD), BF16),
        vmem((2, 2, NV, PAD), BF16),
        vmem((2, 2, NV, PAD), BF16),
        vmem((2, 2, NV, PAD), BF16),
        vmem((2, NF, NV, PAD), BF16),
        vmem((2, Q, NV // 2, 2 * NV), F32),
        vmem((2, NV // 2, 2 * NV), F32),
        vmem((2, 2, NV // 2, 2 * NV), F32),
        vmem((2, NF, NV // 2, 2 * NV), F32),
        pltpu.SemaphoreType.DMA((N_IDS,)),
        pltpu.SemaphoreType.DMA((N_IDS,)),
    ]
    basis = pl.pallas_call(
        kernel,
        out_shape=jax.ShapeDtypeStruct(start_vectors.shape[::-1], F32),
        in_specs=[pl.BlockSpec(memory_space=pltpu.VMEM)] * 3,
        out_specs=pl.BlockSpec(memory_space=pltpu.VMEM),
        scratch_shapes=shapes,
        compiler_params=pltpu.CompilerParams(
            collective_id=0, has_side_effects=True, vmem_limit_bytes=40 * 1024 * 1024
        ),
        cost_estimate=pl.CostEstimate(
            flops=4_000_000_000, bytes_accessed=400_000, transcendentals=200_000
        ),
        name="subspace",
    )(snapshots, spread.reshape(1, -1), start_vectors.T)
    return basis.T


def solution(mesh):
    return jax.shard_map(
        per_device,
        mesh=mesh,
        in_specs=(P("snap", "feat"), P("snap"), P("snap", None)),
        out_specs=P("snap", None),
        check_vma=False,
    )
```

```python
import jax
import jax.numpy as jnp
from jax import lax
from jax.experimental import pallas as pl
from jax.experimental.pallas import tpu as pltpu
from jax.sharding import PartitionSpec as P

Z = 16
Q = 4
NF = 8
NX = 4
HOPS = 4
HALVES = 2
ROWS = 152
PAD = 160
WIDE = 4 * PAD
NARROW = 384
NV = 64
FEATURES = 8192
TOTAL = Z * Q * ROWS
F32 = jnp.float32
BF16 = jnp.bfloat16
HIGHEST = lax.Precision.HIGHEST
R_OFF = (0, 1, 1, 2, 2, 3, 3, 3, 4)
C_OFF = (0, 0, 1, 1, 2, 2, 3, 4, 4)
FEAT_STEPS = ((2, 1), (1, 1), (3, 1), (0, 1), (2, 0), (1, 0), (3, 0))


def dot_nt(a, b, precision=None):
    return lax.dot_general(
        a, b, (((1,), (1,)), ((), ())), precision=precision, preferred_element_type=F32
    )


def dot_nn(a, b, precision=None):
    return lax.dot_general(
        a, b, (((1,), (0,)), ((), ())), precision=precision, preferred_element_type=F32
    )


def eye(n):
    row = lax.broadcasted_iota(jnp.int32, (n, n), 0)
    column = lax.broadcasted_iota(jnp.int32, (n, n), 1)
    return row == column


def column_of(row):
    return jnp.sum(jnp.where(eye(row.shape[1]), row, 0.0), axis=1, keepdims=True)


def row_of(column):
    return jnp.sum(jnp.where(eye(column.shape[0]), column, 0.0), axis=0, keepdims=True)


def inverse_factor(gram):
    n = gram.shape[0]
    on_diagonal = jnp.where(eye(n), gram, 0.0)
    scale_column = lax.rsqrt(jnp.sum(on_diagonal, axis=1, keepdims=True))
    scale_row = lax.rsqrt(jnp.sum(on_diagonal, axis=0, keepdims=True))
    both = jnp.concatenate([gram * scale_column * scale_row, eye(n).astype(F32)], axis=1)
    groups = [both[8 * g : 8 * g + 8] for g in range(n // 8)]
    rows = lax.broadcasted_iota(jnp.int32, (8, 2 * n), 0)
    for j in range(0, n, 2):
        top, r = j // 8, j % 8
        left = {g: jnp.broadcast_to(groups[g][:, j : j + 1], (8, 2 * n)) for g in range(top, n // 8)}
        right = {g: jnp.broadcast_to(groups[g][:, j + 1 : j + 2], (8, 2 * n)) for g in range(top, n // 8)}
        row0, row1 = groups[top][r : r + 1, :], groups[top][r + 1 : r + 2, :]
        a, b, d = left[top][r : r + 1, :], left[top][r + 1 : r + 2, :], right[top][r + 1 : r + 2, :]
        over = 1.0 / (a * d - b * b)
        add0, add1 = (d * row0 - b * row1) * over, (a * row1 - b * row0) * over
        step = b * (1.0 / a) * row0
        for g in range(top, n // 8):
            change = left[g] * add0 + right[g] * add1
            if g == top:
                change = jnp.where(rows > r + 1, change, jnp.where(rows == r + 1, step, 0.0))
            groups[g] = groups[g] - change
    both = jnp.concatenate(groups, axis=0)
    diagonal = jnp.sum(jnp.where(eye(n), both[:, :n], 0.0), axis=1, keepdims=True)
    return both[:, n:] * lax.rsqrt(diagonal) * scale_row


def count_ids():
    sizes = {
        "up": (HOPS + 1) * HALVES,
        "down": (HOPS + 1) * HALVES,
        "across": (HOPS + 1) * HALVES,
        "mate": (HOPS + 1) * HALVES,
        "x": 9,
        "y": 2,
        "gather": 3 * 5,
        "parts": 3 * 4,
        "feat": 3 * 8,
        "gram_q": 2 * 4,
        "gram_z": 2 * 2,
        "gram_f": 2 * 8,
    }
    names, count = {}, 0
    for name, size in sizes.items():
        names[name] = count
        count += size
    return names, count


NAMES, N_IDS = count_ids()


def kernel(
    x_ref,
    spread_ref,
    start_ref,
    out_ref,
    cbuf,
    rbuf,
    pbuf,
    xbuf,
    ysend,
    yrecv,
    keep,
    kq,
    k0,
    width_src,
    width_c,
    width_r,
    width_0,
    w_src,
    w_c,
    w_r,
    w_0,
    d_rsrc,
    d_csrc,
    d_r,
    d_c,
    d_f,
    i_rsrc,
    i_csrc,
    i_r,
    i_c,
    i_f,
    g_q,
    g_zsrc,
    g_z,
    g_f,
    send_sem,
    recv_sem,
):
    snap = lax.axis_index("snap")
    f = lax.axis_index("feat")
    z = snap // Q
    q = snap % Q
    y = q // 2
    c = q % 2
    x = f % NX
    yh = f // NX

    def tile_of(core):
        k = f + 1 if core == 0 else NF - f
        is_7 = (k == 7).astype(jnp.int32)
        return k, (k + 1) // 2 - is_7, k // 2 + is_7

    (k_a, r_off_a, c_off_a), (k_b, r_off_b, c_off_b) = tile_of(0), tile_of(1)
    c_offs = [c_off_a, c_off_b]
    k = k_a + c * (k_b - k_a)
    r_off = r_off_a + c * (r_off_b - r_off_a)
    c_off = c_off_a + c * (c_off_b - c_off_a)
    first = k == 1
    not_first = k != 1
    is_last = k == NF
    from_away = [not_first | (c != i) for i in range(2)]
    half_depth = cbuf.shape[4]
    upper = z >= Z // 2
    last_rows = (y + upper.astype(jnp.int32)) % 2
    member = q * 2 + yh

    def at(zz, yy, cc, ff):
        return {"snap": ((zz + Z) % Z) * Q + yy * 2 + cc, "feat": ff}

    across = at(z, 1 - y, c, f)
    mate = at(z, y, 1 - c, f)
    pending = []

    def copy(src, dst, name, send, recv, device, when=None):
        made = pltpu.make_async_remote_copy(
            src_ref=src,
            dst_ref=dst,
            send_sem=send_sem.at[NAMES[name] + send],
            recv_sem=recv_sem.at[NAMES[name] + recv],
            device_id=device,
            device_id_type=pl.DeviceIdType.MESH,
        )
        if when is None:
            made.start()
        else:
            pl.when(when)(made.start)
        pending.append((made, when))

    marks = [0, 0]

    def settle(everything=False):
        until = len(pending) if everything else marks[1]
        for made, when in pending[marks[0] : until]:
            if when is None:
                made.wait_send()
            else:
                pl.when(when)(made.wait_send)
        marks[0], marks[1] = until, len(pending)

    def arrived(dst, name, recv):
        pltpu.make_async_remote_copy(
            src_ref=dst,
            dst_ref=dst,
            send_sem=send_sem.at[NAMES[name]],
            recv_sem=recv_sem.at[NAMES[name] + recv],
            device_id=mate,
            device_id_type=pl.DeviceIdType.MESH,
        ).wait_recv()

    barrier = pltpu.get_barrier_semaphore()
    near = [at(z + 1, y, c, f), at(z - 1, y, c, f), across, mate]
    near += [at(z, y, c, yh * NX + (x + i) % NX) for i in range(1, NX)]
    near += [at(z, y, c, (f + NX) % NF)]
    for device in near:
        pl.semaphore_signal(
            barrier, inc=1, device_id=device, device_id_type=pl.DeviceIdType.MESH
        )
    for half in range(HALVES):
        part = x_ref[:, half * half_depth : (half + 1) * half_depth]
        rest = jnp.zeros((PAD - ROWS, half_depth), BF16)
        cbuf[0, c, half, :ROWS, :] = part
        cbuf[0, c, half, ROWS:, :] = rest
    lane = lax.broadcasted_iota(jnp.int32, (1, PAD), 1)
    width_src[...] = jnp.broadcast_to(
        jnp.concatenate(
            [spread_ref[...].astype(F32), jnp.ones((1, PAD - ROWS), F32)], axis=1
        ),
        (8, PAD),
    )
    pl.semaphore_wait(barrier, len(near))

    def send_down(h, half):
        src = rbuf.at[h, y, half] if h > 0 else cbuf.at[0, c, half]
        if h < HOPS:
            number = (h + 1) * HALVES + half
            copy(src, rbuf.at[h + 1, y, half], "down", number, number, at(z - 1, y, c, f))
        number = h * HALVES + half
        copy(src, rbuf.at[h, y, half], "across", number, number, across, upper if h == HOPS else None)

    def send_up(h, half):
        src = cbuf.at[h, c, half]
        if h < HOPS:
            number = (h + 1) * HALVES + half
            copy(src, cbuf.at[h + 1, c, half], "up", number, number, at(z + 1, y, c, f))
        number = h * HALVES + half
        copy(src, cbuf.at[h, c, half], "mate", number, number, mate)

    def travel(h, halves=range(HALVES)):
        for half in halves:
            number = h * HALVES + half
            if h > 0:
                arrived(rbuf.at[h, y, half], "down", number)
            send_down(h, half)
            if h > 0:
                arrived(cbuf.at[h, c, half], "up", number)
            send_up(h, half)

    def norms(ref, h, i):
        total = jnp.zeros((PAD, half_depth), F32)
        for half in range(HALVES):
            wide = ref[h, i, half].astype(F32)
            total = total + wide * wide
        return jnp.sum(total, axis=1, keepdims=True)

    known = {}

    def c_norms(h):
        if ("c", h) not in known:
            known["c", h] = [norms(cbuf, h, j) for j in range(2)]
        return known["c", h]

    def r_norms(h, picks):
        if ("r", h) not in known:
            known["r", h] = [row_of(norms(rbuf, h, i)) for i in picks]
        return known["r", h]

    def owner_of(kk):
        place, last = (0, 0) if kk == 0 else ((kk - 1) % NX, (kk - 1) // NX)
        owner = place + c * (NX - 1 - 2 * place)
        return owner, last + c * (1 - 2 * last), 2 if kk == 0 else last

    def tile(ref, kk, *place):
        return ref.at[place + (slice(None), slice(0, NARROW if kk == 8 else WIDE))]

    def make_tile(kk):
        r, h = R_OFF[kk], C_OFF[kk]
        picks = [last_rows] if kk == 8 else [0, 1]
        c_sums, r_sums = c_norms(h), r_norms(r, picks)
        blocks = []
        for j in range(2):
            for n, i in enumerate(picks):
                inner = dot_nt(cbuf[h, j, 0], rbuf[r, i, 0])
                for half in range(1, HALVES):
                    inner = inner + dot_nt(cbuf[h, j, half], rbuf[r, i, half])
                blocks.append(c_sums[j] + r_sums[n] - 2.0 * inner)
        if kk == 8:
            blocks.append(jnp.zeros((PAD, NARROW - 2 * PAD), F32))
        tile(pbuf, kk, kk)[...] = jnp.concatenate(blocks, axis=1).astype(BF16)
        owner, _, slot = owner_of(kk)
        source = (x - owner + NX - 1) % NX % 3
        copy(
            tile(pbuf, kk, kk),
            tile(xbuf, kk, slot, source),
            "x",
            kk,
            slot * 3 + source,
            at(z, y, c, yh * NX + owner),
            x != owner,
        )

    def sum_x(kk):
        owner, last, slot = owner_of(kk)
        kind = 1 if kk == 0 else 0

        @pl.when(x == owner)
        def _():
            for i in range(3):
                arrived(tile(xbuf, kk, slot, i), "x", slot * 3 + i)
            total = tile(pbuf, kk, kk)[...].astype(F32)
            for i in range(3):
                total = total + tile(xbuf, kk, slot, i)[...].astype(F32)

            @pl.when(yh == last)
            def _():
                tile(keep, kk, kind)[...] = total

            @pl.when(yh != last)
            def _():
                tile(ysend, kk, kind)[...] = total.astype(BF16)

        copy(
            tile(ysend, kk, kind),
            tile(yrecv, kk, kind),
            "y",
            kind,
            kind,
            at(z, y, c, (f + NX) % NF),
            (x == owner) & (yh != last),
        )

    def rows_in(h):
        for half in range(HALVES):
            arrived(rbuf.at[h, 1 - y, half], "across", h * HALVES + half)

    def columns_in(h):
        for half in range(HALVES):
            arrived(cbuf.at[h, 1 - c, half], "mate", h * HALVES + half)

    def spread_out(src, c_dst, r_dst, z_dst, base):
        for i in range(2):
            copy(src, r_dst.at[y], "gather", base + i, base + y, at(z - r_off, i, c, f))
        for i in range(2):
            there = at(z + c_offs[i], y, i, f)
            copy(src, c_dst.at[c], "gather", base + 2 + i, base + 2 + c, there, from_away[i])
        copy(src, z_dst.at[y], "gather", base + 4, base + 4, across, first)

        @pl.when(first)
        def _():
            c_dst[c] = src[...]
            z_dst[y] = src[...]

    def spread_in(c_dst, r_dst, z_dst, base):
        for i in range(2):
            arrived(r_dst.at[i], "gather", base + i)
        for i in range(2):
            pl.when(from_away[i])(lambda i=i: arrived(c_dst.at[i], "gather", base + 2 + i))
        pl.when(first)(lambda: arrived(z_dst.at[1 - y], "gather", base + 4))

    travel(0)
    rbuf[0, y] = cbuf[0, c]
    travel(1)
    columns_in(0)
    rows_in(0)
    make_tile(0)
    travel(2)
    rows_in(1)
    make_tile(1)
    columns_in(1)
    make_tile(2)
    travel(3)
    sum_x(0)
    rows_in(2)
    make_tile(3)
    columns_in(2)
    make_tile(4)
    travel(4, range(HALVES // 2))
    rows_in(3)
    make_tile(5)
    columns_in(3)
    make_tile(6)
    travel(4, range(HALVES // 2, HALVES))
    columns_in(4)
    make_tile(7)
    pl.when(upper)(lambda: rows_in(4))
    make_tile(8)
    sum_x(1)
    sum_x(2)
    sum_x(3)
    sum_x(4)
    spread_out(width_src, width_c, width_r, width_0, 0)
    sum_x(5)
    sum_x(6)
    spread_in(width_c, width_r, width_0, 0)
    sum_x(7)
    sum_x(8)

    def kernel_block(kind, b, c_column, r_row, dst, place):
        row = lax.broadcasted_iota(jnp.int32, (PAD, PAD), 0)
        column = lax.broadcasted_iota(jnp.int32, (PAD, PAD), 1)
        inside = (row < ROWS) & (column < ROWS)
        lanes = slice(b * PAD, (b + 1) * PAD)
        distance = keep[kind, :, lanes] + yrecv[kind, :, lanes].astype(F32)
        exponent = -(distance / (c_column * r_row)) / FEATURES
        dst[place] = jnp.where(inside, jnp.exp(exponent), 0.0).astype(BF16)

    c_columns = [column_of(width_c[j, :1, :]) for j in range(2)]

    @pl.when(first)
    def _():
        arrived(yrecv.at[1], "y", 1)
        for b in range(4):
            kernel_block(1, b, c_columns[b // 2], width_0[b % 2, :1, :], k0, b)

    @pl.when(jnp.logical_not(is_last))
    def _():
        arrived(yrecv.at[0], "y", 0)
        for b in range(4):
            kernel_block(0, b, c_columns[b // 2], width_r[b % 2, :1, :], kq, b)

    @pl.when(is_last)
    def _():
        arrived(tile(yrecv, 8, 0), "y", 0)
        for j in range(2):
            kq[2 * j + 1 - last_rows] = jnp.zeros((PAD, PAD), BF16)
            kernel_block(0, j, c_columns[j], width_r[last_rows, :1, :], kq, 2 * j + last_rows)

    def parts_out(index, height, w_of, r_src, c_src, got_r, got_c):
        base = index * 4
        kind = got_r.dtype
        for i in range(2):
            part = dot_nn(w_of("c", 0), kq[i]) + dot_nn(w_of("c", 1), kq[2 + i])
            r_src[i] = part[:height].astype(kind)
            copy(r_src.at[i], got_r.at[y], "parts", base + i, base + y, at(z + r_off, i, c, f))
        for j in range(2):
            part = dot_nt(w_of("r", 0), kq[2 * j]) + dot_nt(w_of("r", 1), kq[2 * j + 1])

            @pl.when(not_first)
            def _(part=part, j=j):
                c_src[j] = part[:height].astype(kind)

            @pl.when(first)
            def _(part=part, j=j):
                own = part + dot_nt(w_of("0", 0), k0[2 * j]) + dot_nt(w_of("0", 1), k0[2 * j + 1])
                c_src[j] = own[:height].astype(kind)

            there = at(z - c_off, y, j, f)
            copy(c_src.at[j], got_c.at[c], "parts", base + 2 + j, base + 2 + c, there, from_away[j])

        @pl.when(first)
        def _():
            got_c[c] = c_src[c]

    def parts_in(index, got_r, got_c):
        base = index * 4
        for i in range(2):
            arrived(got_r.at[i], "parts", base + i)

        for i in range(2):
            pl.when(from_away[i])(lambda i=i: arrived(got_c.at[i], "parts", base + 2 + i))
        total = got_r[0].astype(F32) + got_r[1].astype(F32)
        return total + got_c[0].astype(F32) + got_c[1].astype(F32)

    def feat_out(total, got_f, name, base):
        got_f[f] = total.astype(got_f.dtype)
        for i, (dx, dy) in enumerate(FEAT_STEPS):
            there = (yh + dy) % 2 * NX + (x + dx) % NX
            copy(got_f.at[f], got_f.at[f], name, base + i, base + i, at(z, y, c, there))

    def feat_in(got_f, name, base):
        for i, (dx, dy) in enumerate(FEAT_STEPS):
            source = (yh + dy) % 2 * NX + (x + NX - dx) % NX
            arrived(got_f.at[source], name, base + i)
        total = got_f[0].astype(F32)
        for i in range(1, NF):
            total = total + got_f[i].astype(F32)
        return total

    def gram_q_out(it, mixed):
        gram = dot_nt(mixed, mixed, HIGHEST)
        g_q[it, q] = jnp.concatenate([gram[: NV // 2], gram[NV // 2 :]], axis=1)
        for i in range(1, Q):
            there = (q + i) % Q
            copy(g_q.at[it, q], g_q.at[it, q], "gram_q", 4 * it + i, 4 * it + i, at(z, there // 2, there % 2, f))

    def gram_q_in(it):
        for i in range(1, Q):
            arrived(g_q.at[it, (q + Q - i) % Q], "gram_q", 4 * it + i)
        here = g_q[it, 0]
        for i in range(1, Q):
            here = here + g_q[it, i]
        g_zsrc[it] = here

        @pl.when(member == 0)
        def _():
            g_z[it, 0] = here

        base = 2 * it
        there = at(z - member, y, c, f)
        copy(g_zsrc.at[it], g_z.at[it, 0], "gram_z", base, base, there, member != 0)
        there = at(z + 8 - member, y, c, f)
        copy(g_zsrc.at[it], g_z.at[it, 1], "gram_z", base + 1, base + 1, there)

    def gram_z_in(it):
        pl.when(member != 0)(lambda: arrived(g_z.at[it, 0], "gram_z", 2 * it))
        arrived(g_z.at[it, 1], "gram_z", 2 * it + 1)
        g_f[it, member] = g_z[it, 0] + g_z[it, 1]
        mine = g_f.at[it, member]
        for i in range(1, 8):
            there = (member + i) % 8
            device = at(z, there // 4, there // 2 % 2, there % 2 * NX + x)
            copy(mine, mine, "gram_f", 8 * it + i, 8 * it + i, device)

    def gram_f_in(it):
        for i in range(1, 8):
            arrived(g_f.at[it, (member + 8 - i) % 8], "gram_f", 8 * it + i)
        pair = g_f[it, 0]
        for i in range(1, 8):
            pair = pair + g_f[it, i]
        pair = pair / TOTAL
        return jnp.concatenate([pair[:, :NV], pair[:, NV:]], axis=0)

    ones = jnp.ones((16, PAD), BF16)
    settle()
    parts_out(0, 8, lambda kind, i: ones, d_rsrc, d_csrc, d_r, d_c)
    settle()
    feat_out(parts_in(0, d_r, d_c), d_f, "feat", 0)
    settle()
    degree = feat_in(d_f, "feat", 0)[:1]
    scale = jnp.where(lane < ROWS, 1.0 / jnp.sqrt(jnp.where(lane < ROWS, degree, 1.0)), 0.0)

    def rows_out(it, vectors):
        w_src[it] = (scale * vectors).astype(BF16)
        spread_out(w_src.at[it], w_c.at[it], w_r.at[it], w_0.at[it], 5 * (it + 1))

    def rows_back(it):
        spread_in(w_c.at[it], w_r.at[it], w_0.at[it], 5 * (it + 1))

        def w_of(kind, i):
            return {"c": w_c, "r": w_r, "0": w_0}[kind][it, i]

        parts_out(it + 1, NV, w_of, i_rsrc.at[it], i_csrc.at[it], i_r.at[it], i_c.at[it])

    def sums_out(it):
        feat_out(parts_in(it + 1, i_r.at[it], i_c.at[it]), i_f.at[it], "feat", 8 * (it + 1))

    def image_in(it):
        return feat_in(i_f.at[it], "feat", 8 * (it + 1))

    start = jnp.concatenate([start_ref[...], jnp.zeros((NV, PAD - ROWS), F32)], axis=1)
    rows_out(0, start)
    settle()
    rows_back(0)
    sums_out(0)
    settle()
    mixed = 0.5 * (start + scale * image_in(0))
    rows_out(1, mixed)
    gram_q_out(0, mixed)
    settle()
    gram_q_in(0)
    rows_back(1)
    sums_out(1)
    settle()
    gram_z_in(0)
    mixed = 0.5 * (mixed + scale * image_in(1))
    gram_q_out(1, mixed)
    settle()
    gram_q_in(1)
    settle()
    first_inverse = inverse_factor(gram_f_in(0))
    mixed = dot_nn(first_inverse, mixed, HIGHEST)
    gram_z_in(1)
    settle()
    settle()
    second_gram = dot_nn(first_inverse, dot_nt(gram_f_in(1), first_inverse, HIGHEST), HIGHEST)
    second_inverse = inverse_factor(second_gram)
    out_ref[...] = dot_nn(second_inverse, mixed, HIGHEST)[:, :ROWS]
    settle(everything=True)


def per_device(snapshots, spread, start_vectors):
    half_depth = snapshots.shape[1] // HALVES
    vmem = pltpu.VMEM
    shapes = [
        vmem((HOPS + 1, 2, HALVES, PAD, half_depth), BF16),
        vmem((HOPS + 1, 2, HALVES, PAD, half_depth), BF16),
        vmem((9, PAD, WIDE), BF16),
        vmem((3, 3, PAD, WIDE), BF16),
        vmem((2, PAD, WIDE), BF16),
        vmem((2, PAD, WIDE), BF16),
        vmem((2, PAD, WIDE), F32),
        vmem((4, PAD, PAD), BF16),
        vmem((4, PAD, PAD), BF16),
        vmem((8, PAD), F32),
        vmem((2, 8, PAD), F32),
        vmem((2, 8, PAD), F32),
        vmem((2, 8, PAD), F32),
        vmem((2, NV, PAD), BF16),
        vmem((2, 2, NV, PAD), BF16),
        vmem((2, 2, NV, PAD), BF16),
        vmem((2, 2, NV, PAD), BF16),
        vmem((2, 8, PAD), F32),
        vmem((2, 8, PAD), F32),
        vmem((2, 8, PAD), F32),
        vmem((2, 8, PAD), F32),
        vmem((NF, 8, PAD), F32),
        vmem((2, 2, NV, PAD), BF16),
        vmem((2, 2, NV, PAD), BF16),
        vmem((2, 2, NV, PAD), BF16),
        vmem((2, 2, NV, PAD), BF16),
        vmem((2, NF, NV, PAD), BF16),
        vmem((2, Q, NV // 2, 2 * NV), F32),
        vmem((2, NV // 2, 2 * NV), F32),
        vmem((2, 2, NV // 2, 2 * NV), F32),
        vmem((2, NF, NV // 2, 2 * NV), F32),
        pltpu.SemaphoreType.DMA((N_IDS,)),
        pltpu.SemaphoreType.DMA((N_IDS,)),
    ]
    basis = pl.pallas_call(
        kernel,
        out_shape=jax.ShapeDtypeStruct(start_vectors.shape[::-1], F32),
        in_specs=[pl.BlockSpec(memory_space=pltpu.VMEM)] * 3,
        out_specs=pl.BlockSpec(memory_space=pltpu.VMEM),
        scratch_shapes=shapes,
        compiler_params=pltpu.CompilerParams(
            collective_id=0, has_side_effects=True, vmem_limit_bytes=40 * 1024 * 1024
        ),
        cost_estimate=pl.CostEstimate(
            flops=4_000_000_000, bytes_accessed=400_000, transcendentals=200_000
        ),
        name="subspace",
    )(snapshots, spread.reshape(1, -1), start_vectors.T)
    return basis.T


def solution(mesh):
    return jax.shard_map(
        per_device,
        mesh=mesh,
        in_specs=(P("snap", "feat"), P("snap"), P("snap", None)),
        out_specs=P("snap", None),
        check_vma=False,
    )
```

```python
import jax
import jax.numpy as jnp
from jax import lax
from jax.experimental import pallas as pl
from jax.experimental.pallas import tpu as pltpu
from jax.sharding import PartitionSpec as P

Z = 16
Q = 4
NF = 8
NX = 4
HOPS = 4
HALVES = 2
ROWS = 152
PAD = 160
WIDE = 4 * PAD
NARROW = 384
NV = 64
FEATURES = 8192
TOTAL = Z * Q * ROWS
F32 = jnp.float32
BF16 = jnp.bfloat16
HIGHEST = lax.Precision.HIGHEST
R_OFF = (0, 1, 1, 2, 2, 3, 3, 3, 4)
C_OFF = (0, 0, 1, 1, 2, 2, 3, 4, 4)
FEAT_STEPS = ((2, 1), (1, 1), (3, 1), (0, 1), (2, 0), (1, 0), (3, 0))


def dot_nt(a, b, precision=None):
    return lax.dot_general(
        a, b, (((1,), (1,)), ((), ())), precision=precision, preferred_element_type=F32
    )


def dot_nn(a, b, precision=None):
    return lax.dot_general(
        a, b, (((1,), (0,)), ((), ())), precision=precision, preferred_element_type=F32
    )


def eye(n):
    row = lax.broadcasted_iota(jnp.int32, (n, n), 0)
    column = lax.broadcasted_iota(jnp.int32, (n, n), 1)
    return row == column


def column_of(row):
    return jnp.sum(jnp.where(eye(row.shape[1]), row, 0.0), axis=1, keepdims=True)


def row_of(column):
    return jnp.sum(jnp.where(eye(column.shape[0]), column, 0.0), axis=0, keepdims=True)


def inverse_factor(gram):
    n = gram.shape[0]
    on_diagonal = jnp.where(eye(n), gram, 0.0)
    scale_column = lax.rsqrt(jnp.sum(on_diagonal, axis=1, keepdims=True))
    scale_row = lax.rsqrt(jnp.sum(on_diagonal, axis=0, keepdims=True))
    both = jnp.concatenate([gram * scale_column * scale_row, eye(n).astype(F32)], axis=1)
    groups = [both[8 * g : 8 * g + 8] for g in range(n // 8)]
    rows = lax.broadcasted_iota(jnp.int32, (8, 2 * n), 0)
    for j in range(0, n, 2):
        top, r = j // 8, j % 8
        left = {g: jnp.broadcast_to(groups[g][:, j : j + 1], (8, 2 * n)) for g in range(top, n // 8)}
        right = {g: jnp.broadcast_to(groups[g][:, j + 1 : j + 2], (8, 2 * n)) for g in range(top, n // 8)}
        row0, row1 = groups[top][r : r + 1, :], groups[top][r + 1 : r + 2, :]
        a, b, d = left[top][r : r + 1, :], left[top][r + 1 : r + 2, :], right[top][r + 1 : r + 2, :]
        over = 1.0 / (a * d - b * b)
        add0, add1 = (d * row0 - b * row1) * over, (a * row1 - b * row0) * over
        step = b * (1.0 / a) * row0
        for g in range(top, n // 8):
            change = left[g] * add0 + right[g] * add1
            if g == top:
                change = jnp.where(rows > r + 1, change, jnp.where(rows == r + 1, step, 0.0))
            groups[g] = groups[g] - change
    both = jnp.concatenate(groups, axis=0)
    diagonal = jnp.sum(jnp.where(eye(n), both[:, :n], 0.0), axis=1, keepdims=True)
    return both[:, n:] * lax.rsqrt(diagonal) * scale_row


def count_ids():
    sizes = {
        "up": (HOPS + 1) * HALVES,
        "down": (HOPS + 1) * HALVES,
        "across": (HOPS + 1) * HALVES,
        "mate": (HOPS + 1) * HALVES,
        "x": 9,
        "y": 2,
        "gather": 3 * 5,
        "parts": 3 * 4,
        "feat": 3 * 8,
        "gram_q": 2 * 4,
        "gram_z": 2 * 2,
        "gram_f": 2 * 8,
    }
    names, count = {}, 0
    for name, size in sizes.items():
        names[name] = count
        count += size
    return names, count


NAMES, N_IDS = count_ids()


def kernel(
    x_ref,
    spread_ref,
    start_ref,
    out_ref,
    cbuf,
    rbuf,
    pbuf,
    xbuf,
    ysend,
    yrecv,
    keep,
    kq,
    k0,
    width_src,
    width_c,
    width_r,
    width_0,
    w_src,
    w_c,
    w_r,
    w_0,
    d_rsrc,
    d_csrc,
    d_r,
    d_c,
    d_f,
    i_rsrc,
    i_csrc,
    i_r,
    i_c,
    i_f,
    g_q,
    g_zsrc,
    g_z,
    g_f,
    send_sem,
    recv_sem,
):
    snap = lax.axis_index("snap")
    f = lax.axis_index("feat")
    z = snap // Q
    q = snap % Q
    y = q // 2
    c = q % 2
    x = f % NX
    yh = f // NX

    def tile_of(core):
        k = f + 1 if core == 0 else NF - f
        is_7 = (k == 7).astype(jnp.int32)
        return k, (k + 1) // 2 - is_7, k // 2 + is_7

    (k_a, r_off_a, c_off_a), (k_b, r_off_b, c_off_b) = tile_of(0), tile_of(1)
    c_offs = [c_off_a, c_off_b]
    k = k_a + c * (k_b - k_a)
    r_off = r_off_a + c * (r_off_b - r_off_a)
    c_off = c_off_a + c * (c_off_b - c_off_a)
    first = k == 1
    not_first = k != 1
    is_last = k == NF
    from_away = [not_first | (c != i) for i in range(2)]
    half_depth = cbuf.shape[4]
    upper = z >= Z // 2
    last_rows = (y + upper.astype(jnp.int32)) % 2
    member = q * 2 + yh

    def at(zz, yy, cc, ff):
        return {"snap": ((zz + Z) % Z) * Q + yy * 2 + cc, "feat": ff}

    across = at(z, 1 - y, c, f)
    mate = at(z, y, 1 - c, f)
    pending = []

    def copy(src, dst, name, send, recv, device, when=None):
        made = pltpu.make_async_remote_copy(
            src_ref=src,
            dst_ref=dst,
            send_sem=send_sem.at[NAMES[name] + send],
            recv_sem=recv_sem.at[NAMES[name] + recv],
            device_id=device,
            device_id_type=pl.DeviceIdType.MESH,
        )
        if when is None:
            made.start()
        else:
            pl.when(when)(made.start)
        pending.append((made, when))

    marks = [0, 0]

    def settle(everything=False):
        until = len(pending) if everything else marks[1]
        for made, when in pending[marks[0] : until]:
            if when is None:
                made.wait_send()
            else:
                pl.when(when)(made.wait_send)
        marks[0], marks[1] = until, len(pending)

    def arrived(dst, name, recv):
        pltpu.make_async_remote_copy(
            src_ref=dst,
            dst_ref=dst,
            send_sem=send_sem.at[NAMES[name]],
            recv_sem=recv_sem.at[NAMES[name] + recv],
            device_id=mate,
            device_id_type=pl.DeviceIdType.MESH,
        ).wait_recv()

    barrier = pltpu.get_barrier_semaphore()
    near = [at(z + 1, y, c, f), at(z - 1, y, c, f), across, mate]
    near += [at(z, y, c, yh * NX + (x + i) % NX) for i in range(1, NX)]
    near += [at(z, y, c, (f + NX) % NF)]
    for device in near:
        pl.semaphore_signal(
            barrier, inc=1, device_id=device, device_id_type=pl.DeviceIdType.MESH
        )
    for half in range(HALVES):
        part = x_ref[:, half * half_depth : (half + 1) * half_depth]
        rest = jnp.zeros((PAD - ROWS, half_depth), BF16)
        cbuf[0, c, half, :ROWS, :] = part
        cbuf[0, c, half, ROWS:, :] = rest
    lane = lax.broadcasted_iota(jnp.int32, (1, PAD), 1)
    width_src[...] = jnp.broadcast_to(
        jnp.concatenate(
            [spread_ref[...].astype(F32), jnp.ones((1, PAD - ROWS), F32)], axis=1
        ),
        (8, PAD),
    )
    pl.semaphore_wait(barrier, len(near))

    def send_down(h, half):
        src = rbuf.at[h, y, half] if h > 0 else cbuf.at[0, c, half]
        if h < HOPS:
            number = (h + 1) * HALVES + half
            copy(src, rbuf.at[h + 1, y, half], "down", number, number, at(z - 1, y, c, f))
        number = h * HALVES + half
        copy(src, rbuf.at[h, y, half], "across", number, number, across, upper if h == HOPS else None)

    def send_up(h, half):
        src = cbuf.at[h, c, half]
        if h < HOPS:
            number = (h + 1) * HALVES + half
            copy(src, cbuf.at[h + 1, c, half], "up", number, number, at(z + 1, y, c, f))
        number = h * HALVES + half
        copy(src, cbuf.at[h, c, half], "mate", number, number, mate)

    def travel(h, halves=range(HALVES)):
        for half in halves:
            number = h * HALVES + half
            if h > 0:
                arrived(rbuf.at[h, y, half], "down", number)
            send_down(h, half)
            if h > 0:
                arrived(cbuf.at[h, c, half], "up", number)
            send_up(h, half)

    def norms(ref, h, i):
        total = jnp.zeros((PAD, half_depth), F32)
        for half in range(HALVES):
            wide = ref[h, i, half].astype(F32)
            total = total + wide * wide
        return jnp.sum(total, axis=1, keepdims=True)

    known = {}

    def c_norms(h):
        if ("c", h) not in known:
            known["c", h] = [norms(cbuf, h, j) for j in range(2)]
        return known["c", h]

    def r_norms(h, picks):
        if ("r", h) not in known:
            known["r", h] = [row_of(norms(rbuf, h, i)) for i in picks]
        return known["r", h]

    def owner_of(kk):
        place, last = (0, 0) if kk == 0 else ((kk - 1) % NX, (kk - 1) // NX)
        owner = place + c * (NX - 1 - 2 * place)
        return owner, last + c * (1 - 2 * last), 2 if kk == 0 else last

    def tile(ref, kk, *place):
        return ref.at[place + (slice(None), slice(0, NARROW if kk == 8 else WIDE))]

    def make_tile(kk):
        r, h = R_OFF[kk], C_OFF[kk]
        picks = [last_rows] if kk == 8 else [0, 1]
        c_sums, r_sums = c_norms(h), r_norms(r, picks)
        blocks = []
        for j in range(2):
            for n, i in enumerate(picks):
                inner = dot_nt(cbuf[h, j, 0], rbuf[r, i, 0])
                for half in range(1, HALVES):
                    inner = inner + dot_nt(cbuf[h, j, half], rbuf[r, i, half])
                blocks.append(c_sums[j] + r_sums[n] - 2.0 * inner)
        if kk == 8:
            blocks.append(jnp.zeros((PAD, NARROW - 2 * PAD), F32))
        tile(pbuf, kk, kk)[...] = jnp.concatenate(blocks, axis=1).astype(BF16)
        owner, _, slot = owner_of(kk)
        source = (x - owner + NX - 1) % NX % 3
        copy(
            tile(pbuf, kk, kk),
            tile(xbuf, kk, slot, source),
            "x",
            kk,
            slot * 3 + source,
            at(z, y, c, yh * NX + owner),
            x != owner,
        )

    def sum_x(kk):
        owner, last, slot = owner_of(kk)
        kind = 1 if kk == 0 else 0

        @pl.when(x == owner)
        def _():
            for i in range(3):
                arrived(tile(xbuf, kk, slot, i), "x", slot * 3 + i)
            total = tile(pbuf, kk, kk)[...].astype(F32)
            for i in range(3):
                total = total + tile(xbuf, kk, slot, i)[...].astype(F32)

            @pl.when(yh == last)
            def _():
                tile(keep, kk, kind)[...] = total

            @pl.when(yh != last)
            def _():
                tile(ysend, kk, kind)[...] = total.astype(BF16)

        copy(
            tile(ysend, kk, kind),
            tile(yrecv, kk, kind),
            "y",
            kind,
            kind,
            at(z, y, c, (f + NX) % NF),
            (x == owner) & (yh != last),
        )

    def rows_in(h):
        for half in range(HALVES):
            arrived(rbuf.at[h, 1 - y, half], "across", h * HALVES + half)

    def columns_in(h):
        for half in range(HALVES):
            arrived(cbuf.at[h, 1 - c, half], "mate", h * HALVES + half)

    def spread_out(src, c_dst, r_dst, z_dst, base):
        for i in range(2):
            copy(src, r_dst.at[y], "gather", base + i, base + y, at(z - r_off, i, c, f))
        for i in range(2):
            there = at(z + c_offs[i], y, i, f)
            copy(src, c_dst.at[c], "gather", base + 2 + i, base + 2 + c, there, from_away[i])
        copy(src, z_dst.at[y], "gather", base + 4, base + 4, across, first)

        @pl.when(first)
        def _():
            c_dst[c] = src[...]
            z_dst[y] = src[...]

    def spread_in(c_dst, r_dst, z_dst, base):
        for i in range(2):
            arrived(r_dst.at[i], "gather", base + i)
        for i in range(2):
            pl.when(from_away[i])(lambda i=i: arrived(c_dst.at[i], "gather", base + 2 + i))
        pl.when(first)(lambda: arrived(z_dst.at[1 - y], "gather", base + 4))

    travel(0)
    rbuf[0, y] = cbuf[0, c]
    travel(1)
    columns_in(0)
    rows_in(0)
    make_tile(0)
    travel(2)
    rows_in(1)
    make_tile(1)
    columns_in(1)
    make_tile(2)
    travel(3)
    sum_x(0)
    rows_in(2)
    make_tile(3)
    columns_in(2)
    make_tile(4)
    travel(4, range(HALVES // 2))
    rows_in(3)
    make_tile(5)
    columns_in(3)
    make_tile(6)
    travel(4, range(HALVES // 2, HALVES))
    columns_in(4)
    make_tile(7)
    pl.when(upper)(lambda: rows_in(4))
    make_tile(8)
    sum_x(1)
    sum_x(2)
    sum_x(3)
    sum_x(4)
    spread_out(width_src, width_c, width_r, width_0, 0)
    sum_x(5)
    sum_x(6)
    spread_in(width_c, width_r, width_0, 0)
    sum_x(7)
    sum_x(8)

    def rate(c_column, r_row):
        return -1.0 / (c_column * r_row * FEATURES)

    def kernel_block(kind, b, factor, dst, place):
        row = lax.broadcasted_iota(jnp.int32, (PAD, PAD), 0)
        column = lax.broadcasted_iota(jnp.int32, (PAD, PAD), 1)
        inside = (row < ROWS) & (column < ROWS)
        lanes = slice(b * PAD, (b + 1) * PAD)
        distance = keep[kind, :, lanes] + yrecv[kind, :, lanes].astype(F32)
        dst[place] = jnp.where(inside, jnp.exp(distance * factor), 0.0).astype(BF16)

    c_columns = [column_of(width_c[j, :1, :]) for j in range(2)]

    @pl.when(first)
    def _():
        factors = [rate(c_columns[b // 2], width_0[b % 2, :1, :]) for b in range(4)]
        arrived(yrecv.at[1], "y", 1)
        for b in range(4):
            kernel_block(1, b, factors[b], k0, b)

    @pl.when(jnp.logical_not(is_last))
    def _():
        factors = [rate(c_columns[b // 2], width_r[b % 2, :1, :]) for b in range(4)]
        arrived(yrecv.at[0], "y", 0)
        for b in range(4):
            kernel_block(0, b, factors[b], kq, b)

    @pl.when(is_last)
    def _():
        factors = [rate(c_columns[j], width_r[last_rows, :1, :]) for j in range(2)]
        for j in range(2):
            kq[2 * j + 1 - last_rows] = jnp.zeros((PAD, PAD), BF16)
        arrived(tile(yrecv, 8, 0), "y", 0)
        for j in range(2):
            kernel_block(0, j, factors[j], kq, 2 * j + last_rows)

    def parts_out(index, height, w_of, r_src, c_src, got_r, got_c):
        base = index * 4
        kind = got_r.dtype
        for i in range(2):
            part = dot_nn(w_of("c", 0), kq[i]) + dot_nn(w_of("c", 1), kq[2 + i])
            r_src[i] = part[:height].astype(kind)
            copy(r_src.at[i], got_r.at[y], "parts", base + i, base + y, at(z + r_off, i, c, f))
        for j in range(2):
            part = dot_nt(w_of("r", 0), kq[2 * j]) + dot_nt(w_of("r", 1), kq[2 * j + 1])

            @pl.when(not_first)
            def _(part=part, j=j):
                c_src[j] = part[:height].astype(kind)

            @pl.when(first)
            def _(part=part, j=j):
                own = part + dot_nt(w_of("0", 0), k0[2 * j]) + dot_nt(w_of("0", 1), k0[2 * j + 1])
                c_src[j] = own[:height].astype(kind)

            there = at(z - c_off, y, j, f)
            copy(c_src.at[j], got_c.at[c], "parts", base + 2 + j, base + 2 + c, there, from_away[j])

        @pl.when(first)
        def _():
            got_c[c] = c_src[c]

    def parts_in(index, got_r, got_c):
        base = index * 4
        for i in range(2):
            arrived(got_r.at[i], "parts", base + i)

        for i in range(2):
            pl.when(from_away[i])(lambda i=i: arrived(got_c.at[i], "parts", base + 2 + i))
        total = got_r[0].astype(F32) + got_r[1].astype(F32)
        return total + got_c[0].astype(F32) + got_c[1].astype(F32)

    def feat_out(total, got_f, name, base):
        got_f[f] = total.astype(got_f.dtype)
        for i, (dx, dy) in enumerate(FEAT_STEPS):
            there = (yh + dy) % 2 * NX + (x + dx) % NX
            copy(got_f.at[f], got_f.at[f], name, base + i, base + i, at(z, y, c, there))

    def feat_in(got_f, name, base):
        for i, (dx, dy) in enumerate(FEAT_STEPS):
            source = (yh + dy) % 2 * NX + (x + NX - dx) % NX
            arrived(got_f.at[source], name, base + i)
        total = got_f[0].astype(F32)
        for i in range(1, NF):
            total = total + got_f[i].astype(F32)
        return total

    def gram_q_out(it, mixed):
        gram = dot_nt(mixed, mixed, HIGHEST)
        g_q[it, q] = jnp.concatenate([gram[: NV // 2], gram[NV // 2 :]], axis=1)
        for i in range(1, Q):
            there = (q + i) % Q
            copy(g_q.at[it, q], g_q.at[it, q], "gram_q", 4 * it + i, 4 * it + i, at(z, there // 2, there % 2, f))

    def gram_q_in(it):
        for i in range(1, Q):
            arrived(g_q.at[it, (q + Q - i) % Q], "gram_q", 4 * it + i)
        here = g_q[it, 0]
        for i in range(1, Q):
            here = here + g_q[it, i]
        g_zsrc[it] = here

        @pl.when(member == 0)
        def _():
            g_z[it, 0] = here

        base = 2 * it
        there = at(z - member, y, c, f)
        copy(g_zsrc.at[it], g_z.at[it, 0], "gram_z", base, base, there, member != 0)
        there = at(z + 8 - member, y, c, f)
        copy(g_zsrc.at[it], g_z.at[it, 1], "gram_z", base + 1, base + 1, there)

    def gram_z_in(it):
        pl.when(member != 0)(lambda: arrived(g_z.at[it, 0], "gram_z", 2 * it))
        arrived(g_z.at[it, 1], "gram_z", 2 * it + 1)
        g_f[it, member] = g_z[it, 0] + g_z[it, 1]
        mine = g_f.at[it, member]
        for i in range(1, 8):
            there = (member + i) % 8
            device = at(z, there // 4, there // 2 % 2, there % 2 * NX + x)
            copy(mine, mine, "gram_f", 8 * it + i, 8 * it + i, device)

    def gram_f_in(it):
        for i in range(1, 8):
            arrived(g_f.at[it, (member + 8 - i) % 8], "gram_f", 8 * it + i)
        pair = g_f[it, 0]
        for i in range(1, 8):
            pair = pair + g_f[it, i]
        pair = pair / TOTAL
        return jnp.concatenate([pair[:, :NV], pair[:, NV:]], axis=0)

    ones = jnp.ones((16, PAD), BF16)
    settle()
    parts_out(0, 8, lambda kind, i: ones, d_rsrc, d_csrc, d_r, d_c)
    settle()
    feat_out(parts_in(0, d_r, d_c), d_f, "feat", 0)
    settle()
    degree = feat_in(d_f, "feat", 0)[:1]
    scale = jnp.where(lane < ROWS, 1.0 / jnp.sqrt(jnp.where(lane < ROWS, degree, 1.0)), 0.0)

    def rows_out(it, vectors):
        w_src[it] = (scale * vectors).astype(BF16)
        spread_out(w_src.at[it], w_c.at[it], w_r.at[it], w_0.at[it], 5 * (it + 1))

    def rows_back(it):
        spread_in(w_c.at[it], w_r.at[it], w_0.at[it], 5 * (it + 1))

        def w_of(kind, i):
            return {"c": w_c, "r": w_r, "0": w_0}[kind][it, i]

        parts_out(it + 1, NV, w_of, i_rsrc.at[it], i_csrc.at[it], i_r.at[it], i_c.at[it])

    def sums_out(it):
        feat_out(parts_in(it + 1, i_r.at[it], i_c.at[it]), i_f.at[it], "feat", 8 * (it + 1))

    def image_in(it):
        return feat_in(i_f.at[it], "feat", 8 * (it + 1))

    start = jnp.concatenate([start_ref[...], jnp.zeros((NV, PAD - ROWS), F32)], axis=1)
    rows_out(0, start)
    settle()
    rows_back(0)
    sums_out(0)
    settle()
    mixed = 0.5 * (start + scale * image_in(0))
    rows_out(1, mixed)
    gram_q_out(0, mixed)
    settle()
    gram_q_in(0)
    rows_back(1)
    sums_out(1)
    settle()
    gram_z_in(0)
    mixed = 0.5 * (mixed + scale * image_in(1))
    gram_q_out(1, mixed)
    settle()
    gram_q_in(1)
    settle()
    first_inverse = inverse_factor(gram_f_in(0))
    mixed = dot_nn(first_inverse, mixed, HIGHEST)
    gram_z_in(1)
    settle()
    settle()
    second_gram = dot_nn(first_inverse, dot_nt(gram_f_in(1), first_inverse, HIGHEST), HIGHEST)
    second_inverse = inverse_factor(second_gram)
    out_ref[...] = dot_nn(second_inverse, mixed, HIGHEST)[:, :ROWS]
    settle(everything=True)


def per_device(snapshots, spread, start_vectors):
    half_depth = snapshots.shape[1] // HALVES
    vmem = pltpu.VMEM
    shapes = [
        vmem((HOPS + 1, 2, HALVES, PAD, half_depth), BF16),
        vmem((HOPS + 1, 2, HALVES, PAD, half_depth), BF16),
        vmem((9, PAD, WIDE), BF16),
        vmem((3, 3, PAD, WIDE), BF16),
        vmem((2, PAD, WIDE), BF16),
        vmem((2, PAD, WIDE), BF16),
        vmem((2, PAD, WIDE), F32),
        vmem((4, PAD, PAD), BF16),
        vmem((4, PAD, PAD), BF16),
        vmem((8, PAD), F32),
        vmem((2, 8, PAD), F32),
        vmem((2, 8, PAD), F32),
        vmem((2, 8, PAD), F32),
        vmem((2, NV, PAD), BF16),
        vmem((2, 2, NV, PAD), BF16),
        vmem((2, 2, NV, PAD), BF16),
        vmem((2, 2, NV, PAD), BF16),
        vmem((2, 8, PAD), F32),
        vmem((2, 8, PAD), F32),
        vmem((2, 8, PAD), F32),
        vmem((2, 8, PAD), F32),
        vmem((NF, 8, PAD), F32),
        vmem((2, 2, NV, PAD), BF16),
        vmem((2, 2, NV, PAD), BF16),
        vmem((2, 2, NV, PAD), BF16),
        vmem((2, 2, NV, PAD), BF16),
        vmem((2, NF, NV, PAD), BF16),
        vmem((2, Q, NV // 2, 2 * NV), F32),
        vmem((2, NV // 2, 2 * NV), F32),
        vmem((2, 2, NV // 2, 2 * NV), F32),
        vmem((2, NF, NV // 2, 2 * NV), F32),
        pltpu.SemaphoreType.DMA((N_IDS,)),
        pltpu.SemaphoreType.DMA((N_IDS,)),
    ]
    basis = pl.pallas_call(
        kernel,
        out_shape=jax.ShapeDtypeStruct(start_vectors.shape[::-1], F32),
        in_specs=[pl.BlockSpec(memory_space=pltpu.VMEM)] * 3,
        out_specs=pl.BlockSpec(memory_space=pltpu.VMEM),
        scratch_shapes=shapes,
        compiler_params=pltpu.CompilerParams(
            collective_id=0, has_side_effects=True, vmem_limit_bytes=40 * 1024 * 1024
        ),
        cost_estimate=pl.CostEstimate(
            flops=4_000_000_000, bytes_accessed=400_000, transcendentals=200_000
        ),
        name="subspace",
    )(snapshots, spread.reshape(1, -1), start_vectors.T)
    return basis.T


def solution(mesh):
    return jax.shard_map(
        per_device,
        mesh=mesh,
        in_specs=(P("snap", "feat"), P("snap"), P("snap", None)),
        out_specs=P("snap", None),
        check_vma=False,
    )
```
